32 devices in a mesh: groups: 2 (over x), blk: 16 (over z, y, core).
Axes of the slice: x: 2, y: 2, z: 4, core: 2. Of those that a mesh axis runs over, the one named last changes fastest.
Arguments:
- state_now: float32 [5, 64, 16384], P(None, None, ('groups', 'blk')), parts along dimension 2, may hold values from -6 to 6
- time_source: float32 [5, 64, 16384], P(None, None, ('groups', 'blk')), parts along dimension 2, may hold values from -6 to 6
- viscosity: float32 [64, 16384], P(None, ('groups', 'blk')), parts along dimension 1, may hold values from 0.05 to 0.5
- advection: float32 [5], replicated, may hold values from 0.2 to 1
- coupling: float32 [5, 5], replicated, may hold values from -2.5 to 2.5
- owner_list: int32 [16384, 1], P(('groups', 'blk')), parts along dimension 0, may hold values from 0 to 15; in each aligned block of 512 rows (0 to 511, 512 to 1023, ...) at most 64 rows name the same one
- owner_offset: int32 [16384], P(('groups', 'blk')), parts along dimension 0, may hold values from 0 to 510
- intersection_weight: float32 [16384], P(('groups', 'blk')), parts along dimension 0, may hold values from 0 to 1
- phase_index: int32 [32], P(('groups', 'blk')), parts along dimension 0, may hold values from 0 to 511
Outputs:
- state_next: float32 [5, 64, 16384], P(None, None, ('groups', 'blk')), parts along dimension 2
The draws below stay inside these ranges and needn't reach their ends.
There are 2 independent parts, one for each index of `groups`. The reference program is written for one: setup_inputs(seed, part) draws one part's arguments, and reference() takes and returns one part's arrays. A program takes and returns all parts, laid end to end along the dimension named above; an argument that names none is the same for every part. Nothing has to cross between parts.
Inputs may be any that keep to these rules, and one draw needn't show every extreme that they name: `owner_list`: within the 512 ghost cells of one block, no owner block is named more than 64 times, a bound that some block reaches.
All inputs are finite; a program needn't handle non-finite values.
Results may differ from the reference program's by a relative error of at most 0.0001.
Values sent between devices are 32-bit elements; how exact they have to be, the bound alone decides.
No kernel may reach another device: no remote copies, remote signals or barrier semaphores. Data moves between devices by JAX's collectives and lax.ppermute only.
A program may use at most 64 MiB of HBM per device.

```python
import math
import jax
import jax.numpy as jnp
import numpy as np
from jax import lax

FIELDS = 5
HARM = 8
PHASES = 512
LAG = 37
ITERS = 4
NJ = 64
NI = 512
CAP = 64
COLS = 8192
N_BLK = 16


def with_ends(entries, own_key, low, high):
    dims = entries.shape
    place = [jax.random.randint(jax.random.fold_in(own_key, axis), (), 0, dims[axis]) for axis in range(len(dims))]
    entries = entries.at[tuple(place)].set(low)
    longest = dims.index(max(dims))
    place[longest] = (place[longest] + 1) % dims[longest]
    return entries.at[tuple(place)].set(high)


def steps_of(rng, dims, cuts, smallest, high):
    gain = 1.0
    for axis_at, shards_of in cuts:
        heights = jax.random.uniform(jax.random.fold_in(jax.random.fold_in(rng, 6), axis_at), (shards_of,), jnp.float32, smallest / len(cuts), high / len(cuts))
        gain = gain * jnp.repeat(jnp.exp(heights), dims[axis_at] // shards_of).reshape((-1,) + (1,) * (len(dims) - 1 - axis_at))
    return gain


def routed_block(rng, own, number, rows, amount, top, most, lean):
    order = jax.random.permutation(rng, amount)
    heavy_load, common = load_shares(amount, rows * top, most, lean, True), load_shares(amount, rows * top, most, lean, False)
    places = jnp.arange(amount)

    def named(lengths, offset_by):
        used = int((lengths > 0).sum())
        fixed = max(1, used // 4)
        moved = fixed + (places - fixed + offset_by * (used - fixed)) % max(1, amount - fixed)
        return jnp.zeros((amount,), jnp.int32).at[order[jnp.where(places < fixed, places, moved)]].set(jnp.asarray(lengths, jnp.int32))

    lengths = jnp.where(number % 4 == 0, named(heavy_load, number // 4), named(common, number - number // 4 - 1))
    mixed = jax.random.permutation(jax.random.fold_in(own, 3), amount)
    donor, sink = mixed[0:amount // 2 * 2:2], mixed[1:amount // 2 * 2:2]
    room = jnp.minimum(lengths[donor] - 1, most - lengths[sink]) // 2
    room = jnp.where((donor == order[0]) | (sink == order[0]) | (lengths[sink] == 0), 0, jnp.maximum(room, 0))
    moved = jax.random.randint(jax.random.fold_in(own, 4), (amount // 2,), 0, 1 << 20) % (room + 1)
    lengths = lengths.at[donor].add(-moved).at[sink].add(moved)
    items = jnp.searchsorted(jnp.cumsum(lengths), jnp.arange(rows * top), side="right").astype(jnp.int32)
    table = items.reshape(top, rows).T
    table = table[jax.random.permutation(jax.random.fold_in(own, 1), rows)]
    offset_by = jax.random.randint(jax.random.fold_in(own, 2), (rows, 1), 0, top)
    return jnp.take_along_axis(table, (jnp.arange(top)[None, :] + offset_by) % top, axis=1)


def load_shares(number_of, total, bound, lean, full):
    portions = [(1 << 20) // math.isqrt(standing ** lean) + 1 for standing in range(1, number_of + 1)]
    largest = bound if full else min(bound, max(-(-total // number_of), total * portions[0] // sum(portions)))
    least = 1 if total - largest >= number_of - 1 else 0
    holding, surplus = [largest] + [least] * (number_of - 1), total - largest - least * (number_of - 1)
    while surplus > 0:
        candidates = [i for i in range(1, number_of) if holding[i] < largest] or [i for i in range(1, number_of) if holding[i] < bound]
        pool, remaining = sum([portions[i] for i in candidates]), surplus
        for i in candidates:
            addition = min(bound - holding[i], max(1, remaining * portions[i] // pool), surplus)
            holding[i] = holding[i] + addition
            surplus = surplus - addition
    return np.array(holding)


def centred(stream_key, extent, spread, most, pieces=(), kind=jnp.bfloat16):
    entries = jax.random.normal(stream_key, extent, jnp.float32) * spread
    if len(pieces) > 0:
        entries = steps_of(stream_key, extent, pieces, -0.22, 0.18) * entries
    return jnp.clip(entries, min=-most, max=most).astype(kind)


def setup_inputs(seed: int = 0, part: int = 0) -> dict:
    key_list = jax.random.split(jax.random.key(seed), 10)
    own_keys = jax.random.split(jax.random.fold_in(key_list[9], part), 10)
    state_now = centred(own_keys[0], (FIELDS, NJ, COLS), 1.0, 6.0, ((2, 16),), jnp.float32)
    time_source = centred(own_keys[1], (FIELDS, NJ, COLS), 1.0, 6.0, ((2, 16),), jnp.float32)
    viscosity = jnp.clip(jnp.exp(math.log(0.5) - 2.3025851 * jax.random.uniform(own_keys[2], (NJ, COLS), jnp.float32) ** steps_of(own_keys[2], (NJ, COLS), ((1, 16),), -0.2, 0.2)), 0.05, 0.5)
    advection = jnp.clip(jnp.exp(jax.random.uniform(key_list[3], (FIELDS,), jnp.float32, math.log(0.2), math.log(1.0))), 0.2, 1.0)
    coupling = centred(key_list[4], (FIELDS, FIELDS), FIELDS ** -0.5, 2.5, (), jnp.float32)
    owner_list_keys = jax.random.split(jax.random.fold_in(own_keys[5], 1), COLS // NI)
    owner_list_turns = jax.random.permutation(jax.random.fold_in(own_keys[5], 3), COLS // NI)
    owner_list = jax.vmap(lambda own, number: routed_block(jax.random.fold_in(own_keys[5], 2), own, number, NI, N_BLK, 1, CAP, 2))(owner_list_keys, owner_list_turns).reshape((COLS, 1))
    owner_offset = with_ends(jax.random.randint(own_keys[6], (COLS,), 0, NI - 1), jax.random.fold_in(own_keys[6], 1), 0, (NI - 1) - 1).astype(jnp.int32)
    intersection_weight = jnp.clip(1.0 * jax.random.uniform(own_keys[7], (COLS,), jnp.float32) ** steps_of(own_keys[7], (COLS,), ((0, 16),), -0.2, 0.2), 0.0, 1.0)
    phase_index = with_ends(jax.random.randint(own_keys[8], (N_BLK,), 0, PHASES), jax.random.fold_in(own_keys[8], 1), 0, PHASES - 1).astype(jnp.int32)
    return {"state_now": state_now, "time_source": time_source, "viscosity": viscosity, "advection": advection, "coupling": coupling, "owner_list": owner_list, "owner_offset": owner_offset, "intersection_weight": intersection_weight, "phase_index": phase_index}


pseudo_step = 0.2


def stencil(block, lower, upper, viscosity, advection, coupling):
    column = jnp.concatenate([lower[:, None, :], block, upper[:, None, :]], axis=1)
    padded = jnp.pad(block, ((0, 0), (0, 0), (1, 1)))
    before = padded[:, :, :-2]
    after = padded[:, :, 2:]
    diffuse = 4.0 * block - column[:, :-2, :] - column[:, 2:, :] - before - after
    mixing = jnp.einsum("cd,djn->cjn", coupling, block, precision=lax.Precision.HIGHEST)
    return advection[:, None, None] * (block - before) + viscosity[None] * diffuse + mixing


def update(block, source, lower, upper, viscosity, advection, coupling):
    change = 1.5 * block + source + stencil(block, lower, upper, viscosity, advection, coupling)
    return block - pseudo_step * change


def harmonic_terms(phase_index, count):
    angle = phase_index.astype(jnp.float32) * (2.0 * math.pi / PHASES)
    orders = jnp.arange(1, HARM + 1, dtype=jnp.float32)
    product = angle[:, None] * orders[None, :]
    ones = jnp.ones_like(angle)[:, None]
    return jnp.concatenate([ones, 2.0 * jnp.cos(product), 2.0 * jnp.sin(product)], axis=1) / count


def harmonic_basis(phase_index):
    angle = (phase_index.astype(jnp.float32) + LAG) * (2.0 * math.pi / PHASES)
    orders = jnp.arange(1, HARM + 1, dtype=jnp.float32)
    product = angle[:, None] * orders[None, :]
    ones = jnp.ones_like(angle)[:, None]
    return jnp.concatenate([ones, jnp.cos(product), jnp.sin(product)], axis=1)


def reference(state_now, time_source, viscosity, advection, coupling, owner_list, owner_offset, intersection_weight, phase_index):
    state = state_now.reshape(FIELDS, NJ, N_BLK, NI).transpose(2, 0, 1, 3)
    source = time_source.reshape(FIELDS, NJ, N_BLK, NI).transpose(2, 0, 1, 3)
    visc_blocks = viscosity.reshape(NJ, N_BLK, NI).transpose(1, 0, 2)
    owners = owner_list[:, 0]
    weights = intersection_weight.reshape(N_BLK, 1, NI)
    terms = harmonic_terms(phase_index, N_BLK)
    basis = harmonic_basis(phase_index)
    stepper = jax.vmap(update, in_axes=(0, 0, 0, 0, 0, None, None))
    for iteration in range(ITERS):
        top_face = state[:, :, NJ - 1, :]
        first = top_face[owners, :, owner_offset].reshape(N_BLK, NI, FIELDS).transpose(0, 2, 1)
        second = top_face[owners, :, owner_offset + 1].reshape(N_BLK, NI, FIELDS).transpose(0, 2, 1)
        lower = weights * first + (1.0 - weights) * second
        bottom_face = state[:, :, 0, :]
        coef = jnp.einsum("ph,pcn->hcn", terms, bottom_face, precision=lax.Precision.HIGHEST)
        upper = jnp.einsum("qh,hcn->qcn", basis, coef, precision=lax.Precision.HIGHEST)
        state = stepper(state, source, lower, upper, visc_blocks, advection, coupling)
    return state.transpose(1, 2, 0, 3).reshape(FIELDS, NJ, N_BLK * NI)
```

```python
import functools
import math

import jax
import jax.numpy as jnp
from jax import lax
from jax.experimental import pallas as pl
from jax.experimental.pallas import tpu as pltpu
from jax.sharding import PartitionSpec as P

HARM = 8
PHASES = 512
LAG = 37
ITERS = 4
PSEUDO = 0.2
LANES = 128
SUB = 8
EXACT = lax.Precision.HIGHEST


class Sizes:
    def __init__(self, fields, rows, width, blocks):
        self.fields, self.rows, self.width, self.blocks = fields, rows, width, blocks
        self.groups = width // LANES
        self.cap = 2 * width // blocks
        self.packs = LANES // self.cap
        self.tops = 0
        self.bottoms = self.tops + ITERS * fields * self.groups
        self.visc = self.bottoms + ITERS * fields * self.groups
        self.slot = self.visc + 4 * self.groups
        self.offsets = self.slot + self.groups
        self.weights = self.offsets + SUB
        self.terms = self.weights + SUB
        self.basis = self.terms + 1
        self.table = -(-(self.basis + 1) // SUB) * SUB


def matrix_of(sz, advection, coupling):
    own = [[-PSEUDO * coupling[c, d] for d in range(sz.fields)] for c in range(sz.fields)]
    speed = [PSEUDO * advection[c] for c in range(sz.fields)]
    for c in range(sz.fields):
        own[c][c] = own[c][c] + ((1.0 - 1.5 * PSEUDO) - speed[c])
    return own, speed


def shifted_west(u):
    lane = lax.broadcasted_iota(jnp.int32, u.shape, 1)
    return jnp.where(lane == 0, 0.0, pltpu.roll(u, 1, axis=1))


def shifted_east(u):
    width = u.shape[1]
    lane = lax.broadcasted_iota(jnp.int32, u.shape, 1)
    return jnp.where(lane == width - 1, 0.0, pltpu.roll(u, width - 1, axis=1))


def advance(sz, own, speed, u, visc, column, source):
    out = []
    for c in range(sz.fields):
        west, east = shifted_west(u[c]), shifted_east(u[c])
        new = speed[c] * west + visc * (west + east + column(c) - 4.0 * u[c])
        for d in range(sz.fields):
            new = new + own[c][d] * u[d]
        if source is not None:
            new = new - source(c)
        out.append(new)
    return out


def edge_column(u, ghost, at_low):
    row = lax.broadcasted_iota(jnp.int32, u.shape, 0)
    up, down = pltpu.roll(u, 1, axis=0), pltpu.roll(u, SUB - 1, axis=0)
    if at_low:
        return jnp.where(row == 0, ghost, up) + down
    return up + jnp.where(row == SUB - 1, ghost, down)


def prepare_kernel(
    sz, adv_ref, coup_ref, phase_ref, low_u, high_u, low_q, high_q, low_v, high_v, owner_ref, offset_ref, weight_ref, out_ref
):
    own, speed = matrix_of(sz, adv_ref, coup_ref)

    def put(at, row):
        for g in range(sz.groups):
            out_ref[at + g : at + g + 1, :] = row[:, g * LANES : (g + 1) * LANES]

    out_ref[sz.basis : sz.table, :] = jnp.zeros((sz.table - sz.basis, LANES), jnp.float32)
    for side, (u_ref, q_ref, v_ref, at_low) in enumerate(
        ((high_u, high_q, high_v, False), (low_u, low_q, low_v, True))
    ):
        face = 0 if at_low else SUB - 1
        inner = 1 if at_low else SUB - 2
        base = sz.bottoms if at_low else sz.tops
        visc = PSEUDO * v_ref[...]
        put(sz.visc + (2 * side) * sz.groups, visc[face : face + 1])
        put(sz.visc + (2 * side + 1) * sz.groups, visc[inner : inner + 1])
        u = [u_ref[c] for c in range(sz.fields)]
        q = [PSEUDO * q_ref[c] for c in range(sz.fields)]
        for k in range(ITERS):
            for c in range(sz.fields):
                put(base + (k * sz.fields + c) * sz.groups, u[c][face : face + 1])
            if k < ITERS - 1:
                u = advance(sz, own, speed, u, visc, lambda c: edge_column(u[c], 0.0, at_low), lambda c: q[c])

    owner, offset, weight = owner_ref[...], offset_ref[...], weight_ref[...]
    member = lax.broadcasted_iota(jnp.int32, (sz.blocks, sz.width), 0) == owner
    member = member.astype(jnp.bfloat16)
    before = lax.broadcasted_iota(jnp.int32, (sz.width, sz.width), 0) <= lax.broadcasted_iota(
        jnp.int32, (sz.width, sz.width), 1
    )
    count = jnp.dot(member, before.astype(jnp.bfloat16), preferred_element_type=jnp.float32)
    rank = jnp.sum(count * member.astype(jnp.float32), axis=0, keepdims=True) - 1.0
    rank = rank.astype(jnp.int32)
    slot = owner * sz.cap + rank
    put(sz.slot, slot.astype(jnp.float32))
    place = (lax.broadcasted_iota(jnp.int32, (LANES, sz.width), 0) == slot % LANES).astype(jnp.float32)
    held = lax.broadcasted_iota(jnp.int32, (SUB, sz.width), 0) == slot // LANES
    values = jnp.concatenate(
        [jnp.where(held, offset.astype(jnp.float32), 0.0), jnp.where(held, weight, 0.0)], axis=0
    )
    tables = lax.dot_general(
        values, place, (((1,), (1,)), ((), ())), precision=EXACT, preferred_element_type=jnp.float32
    )
    out_ref[sz.offsets : sz.offsets + 2 * SUB, :] = tables

    order = lax.broadcasted_iota(jnp.int32, (1, LANES), 1)
    harmonic = jnp.where(order > HARM, order - HARM, order).astype(jnp.float32)
    used = order <= 2 * HARM

    def waves(angle):
        product = angle * harmonic
        return jnp.where(order <= HARM, jnp.cos(product), jnp.sin(product))

    phase = phase_ref[0].astype(jnp.float32)
    scale = jnp.where(order == 0, 1.0, 2.0) / sz.blocks
    terms = waves(phase * (2.0 * math.pi / PHASES)) * scale
    basis = waves((phase + LAG) * (2.0 * math.pi / PHASES))
    out_ref[sz.terms : sz.terms + 1, :] = jnp.where(used, terms, 0.0)
    out_ref[sz.basis : sz.basis + 1, :] = jnp.where(used, basis, 0.0)


def interior_kernel(sz, adv_ref, coup_ref, u_ref, q_ref, v_ref, out_ref, work):
    own, speed = matrix_of(sz, adv_ref, coup_ref)
    tiles = sz.rows // SUB
    row = lax.broadcasted_iota(jnp.int32, (SUB, sz.width), 0)
    for k in range(ITERS):
        src = u_ref if k == 0 else work.at[(k - 1) % 2]
        dst = out_ref if k == ITERS - 1 else work.at[k % 2]
        for t in range(tiles):
            here = slice(t * SUB, (t + 1) * SUB)
            u = [src[c, here, :] for c in range(sz.fields)]

            def column(c):
                up, down = pltpu.roll(u[c], 1, axis=0), pltpu.roll(u[c], SUB - 1, axis=0)
                above = src[c, t * SUB - 1 : t * SUB, :] if t > 0 else 0.0
                below = src[c, (t + 1) * SUB : (t + 1) * SUB + 1, :] if t < tiles - 1 else 0.0
                return jnp.where(row == 0, above, up) + jnp.where(row == SUB - 1, below, down)

            new = advance(sz, own, speed, u, PSEUDO * v_ref[here, :], column, lambda c: PSEUDO * q_ref[c, here, :])
            for c in range(sz.fields):
                dst[c, here, :] = new[c]


def couple_kernel(
    sz,
    adv_ref,
    coup_ref,
    me_ref,
    even_ref,
    odd_ref,
    low_u,
    high_u,
    low_q,
    high_q,
    low_v,
    high_v,
    out_ref,
    slot_offset,
    slot_weight,
    slot_value,
    top_ref,
    next_ref,
    lower_ref,
    bottom_ref,
):
    own, speed = matrix_of(sz, adv_ref, coup_ref)
    me = me_ref[0]
    packs, groups, fields = sz.packs, sz.groups, sz.fields
    stride = packs // 2 * sz.table
    lane = lax.broadcasted_iota(jnp.int32, (SUB, LANES), 1)

    def line(b, row):
        ref = (even_ref, odd_ref)[b % 2]
        return ref[pl.ds(b // 2 * sz.table + row, SUB, stride=stride), :]

    def wide(b, row):
        return jnp.concatenate([line(b, row + g) for g in range(groups)], axis=1)

    for m in range(SUB):
        offsets = [line(b, sz.offsets + m) for b in range(packs)]
        weights = [line(b, sz.weights + m) for b in range(packs)]
        for n in range(packs):
            tile_o, tile_w = offsets[n], weights[n]
            for b in range(packs):
                if b != n:
                    mine = lane // sz.cap == b
                    turn = (b - n) * sz.cap % LANES
                    tile_o = jnp.where(mine, pltpu.roll(offsets[b], turn, axis=1), tile_o)
                    tile_w = jnp.where(mine, pltpu.roll(weights[b], turn, axis=1), tile_w)
            o = jnp.bitwise_xor(m * packs + n, me)
            slot_offset[o] = tile_o.astype(jnp.int32)
            slot_weight[o] = tile_w

    slots = [wide(b, sz.slot).astype(jnp.int32) for b in range(packs)]
    takers = [jnp.bitwise_xor(s // sz.cap, me) for s in slots]
    places = [s % sz.cap + b * sz.cap for b, s in enumerate(slots)]
    basis = jnp.concatenate([line(b, sz.basis) for b in range(packs)], axis=0)
    terms = jnp.concatenate([line(b, sz.terms) for b in range(packs)], axis=0)
    kernel = lax.dot_general(
        basis, terms, (((1,), (1,)), ((), ())), precision=EXACT, preferred_element_type=jnp.float32
    )

    def gather(tiles):
        def first_stage(o, carry):
            offset, weight = slot_offset[o], slot_weight[o]
            at, part = offset % LANES, offset // LANES
            for c in range(fields):
                pair = []
                for ref in (top_ref, next_ref):
                    value = None
                    for g in range(groups):
                        source = jnp.broadcast_to(ref[g, o, c : c + 1, :], (SUB, LANES))
                        taken = jnp.take_along_axis(source, at, axis=1)
                        value = taken if value is None else jnp.where(part == g, taken, value)
                    pair.append(value)
                slot_value[o, c] = weight * pair[0] + (1.0 - weight) * pair[1]
            return carry

        lax.fori_loop(0, sz.blocks, first_stage, 0, unroll=2)
        for b in tiles:
            for g in range(groups):
                cells = slice(g * LANES, (g + 1) * LANES)
                taker, place = takers[b][:, cells], places[b][:, cells]

                def second_stage(o, found):
                    mine = taker == o
                    return tuple(
                        jnp.where(mine, jnp.take_along_axis(slot_value[o, c], place, axis=1), found[c])
                        for c in range(fields)
                    )

                zero = jnp.zeros((SUB, LANES), jnp.float32)
                found = lax.fori_loop(0, sz.blocks, second_stage, (zero,) * fields, unroll=4)
                for c in range(fields):
                    lower_ref[b, c, :, cells] = found[c]

    def face_step(e, visc, extra):
        return advance(sz, own, speed, e, visc, extra, None)

    visc = {}
    for b in range(packs):
        for n, name in enumerate(("top", "top_in", "bottom", "bottom_in")):
            visc[name, b] = wide(b, sz.visc + n * groups)

    blocks = range(packs)
    outer = {}
    inner = {}
    state = {True: [low_u[c] for c in range(fields)], False: [high_u[c] for c in range(fields)]}
    sources = {True: low_q, False: high_q}
    viscs = {True: PSEUDO * low_v[...], False: PSEUDO * high_v[...]}
    for k in range(ITERS):
        for b in blocks:
            for c in range(fields):
                top = wide(b, sz.tops + (k * fields + c) * groups)
                bottom = wide(b, sz.bottoms + (k * fields + c) * groups)
                if k > 0:
                    top, bottom = top + outer["top", b][c], bottom + outer["bottom", b][c]
                rows = pl.ds(b * SUB + c, SUB, stride=packs * SUB)
                after = pltpu.roll(top, sz.width - 1, axis=1)
                for g in range(groups):
                    cells = slice(g * LANES, (g + 1) * LANES)
                    top_ref.reshape(groups, sz.blocks * SUB, LANES)[g, rows, :] = top[:, cells]
                    next_ref.reshape(groups, sz.blocks * SUB, LANES)[g, rows, :] = after[:, cells]
                bottom_ref[c, b * SUB : (b + 1) * SUB, :] = bottom
        gather(blocks if k < ITERS - 1 else blocks[:1])
        upper = [
            jnp.dot(kernel, bottom_ref[c], precision=EXACT, preferred_element_type=jnp.float32) for c in range(fields)
        ]
        if k < ITERS - 1:
            for b in blocks:
                ghosts = {
                    "top": [upper[c][b * SUB : (b + 1) * SUB] for c in range(fields)],
                    "bottom": [lower_ref[b, c] for c in range(fields)],
                }
                for name, ghost in ghosts.items():
                    v, v_in = visc[name, b], visc[name + "_in", b]
                    if k == 0:
                        outer[name, b] = [v * ghost[c] for c in range(fields)]
                    else:
                        e, e_in = outer[name, b], inner.get((name, b))
                        inner[name, b] = [v_in * e[c] for c in range(fields)]
                        outer[name, b] = face_step(
                            e, v, lambda c: ghost[c] if e_in is None else ghost[c] + e_in[c]
                        )
        for at_low in (True, False):
            u, q = state[at_low], sources[at_low]
            ghost = [(lower_ref[0, c] if at_low else upper[c])[0:1] for c in range(fields)]
            state[at_low] = advance(
                sz, own, speed, u, viscs[at_low], lambda c: edge_column(u[c], ghost[c], at_low), lambda c: PSEUDO * q[c]
            )
    for c in range(fields):
        out_ref[0, c] = state[True][c]
        out_ref[1, c] = state[False][c]


def spread(table, blocks):
    parts = [table]
    bit = 2
    while bit < blocks:
        masks = [bit] if bit == 2 or 2 * bit >= blocks else [bit, 2 * bit, 3 * bit]
        have = jnp.concatenate(parts, axis=0)
        parts = [have] + [lax.ppermute(have, "blk", [(i, i ^ m) for i in range(blocks)]) for m in masks]
        bit = bit * (len(masks) + 1)
    even = jnp.concatenate(parts, axis=0)
    odd = lax.ppermute(even, "blk", [(i, i ^ 1) for i in range(blocks)])
    return even, odd


def per_device(
    state_now,
    time_source,
    viscosity,
    advection,
    coupling,
    owner_list,
    owner_offset,
    intersection_weight,
    phase_index,
):
    blocks = lax.axis_size("blk")
    fields, rows, width = state_now.shape
    sz = Sizes(fields, rows, width, blocks)
    me = lax.axis_index("blk").astype(jnp.int32).reshape(1)
    smem = pl.BlockSpec(memory_space=pltpu.SMEM)
    vmem = pl.BlockSpec(memory_space=pltpu.VMEM)
    ends = [
        pl.BlockSpec((fields, SUB, width), lambda i: (0, 0, 0)),
        pl.BlockSpec((fields, SUB, width), lambda i: (0, rows // SUB - 1, 0)),
    ]
    visc_ends = [
        pl.BlockSpec((SUB, width), lambda i: (0, 0)),
        pl.BlockSpec((SUB, width), lambda i: (rows // SUB - 1, 0)),
    ]
    edges = [state_now, state_now, time_source, time_source, viscosity, viscosity]
    line = pl.BlockSpec((1, width), lambda i: (0, 0))
    limit = pltpu.CompilerParams(vmem_limit_bytes=50 * 1024 * 1024)
    table = pl.pallas_call(
        functools.partial(prepare_kernel, sz),
        grid=(1,),
        out_shape=jax.ShapeDtypeStruct((sz.table, LANES), jnp.float32),
        in_specs=[smem, smem, smem] + ends + ends + visc_ends + [line] * 3,
        out_specs=pl.BlockSpec((sz.table, LANES), lambda i: (0, 0)),
        compiler_params=limit,
    )(
        advection,
        coupling,
        phase_index,
        *edges,
        owner_list.reshape(1, width),
        owner_offset.reshape(1, width),
        intersection_weight.reshape(1, width),
    )
    even, odd = spread(table, blocks)
    inside = pl.pallas_call(
        functools.partial(interior_kernel, sz),
        out_shape=jax.ShapeDtypeStruct((fields, rows, width), jnp.float32),
        in_specs=[smem, smem, vmem, vmem, vmem],
        out_specs=vmem,
        scratch_shapes=[pltpu.VMEM((2, fields, rows, width), jnp.float32)],
        compiler_params=limit,
    )(advection, coupling, state_now, time_source, viscosity)
    whole = pl.BlockSpec((blocks // 2 * sz.table, LANES), lambda i: (0, 0))
    strips = pl.pallas_call(
        functools.partial(couple_kernel, sz),
        grid=(1,),
        out_shape=jax.ShapeDtypeStruct((2, fields, SUB, width), jnp.float32),
        in_specs=[smem, smem, smem, whole, whole] + ends + ends + visc_ends,
        out_specs=pl.BlockSpec((2, fields, SUB, width), lambda i: (0, 0, 0, 0)),
        scratch_shapes=[
            pltpu.VMEM((blocks, SUB, LANES), jnp.int32),
            pltpu.VMEM((blocks, SUB, LANES), jnp.float32),
            pltpu.VMEM((blocks, fields, SUB, LANES), jnp.float32),
            pltpu.VMEM((sz.groups, blocks, SUB, LANES), jnp.float32),
            pltpu.VMEM((sz.groups, blocks, SUB, LANES), jnp.float32),
            pltpu.VMEM((sz.packs, fields, SUB, width), jnp.float32),
            pltpu.VMEM((fields, blocks, width), jnp.float32),
        ],
        compiler_params=limit,
    )(advection, coupling, me, even, odd, *edges)
    half = SUB // 2
    return jnp.concatenate([strips[0, :, :half], inside[:, half : rows - half], strips[1, :, half:]], axis=1)


def solution(mesh):
    return jax.shard_map(
        per_device,
        mesh=mesh,
        in_specs=(
            P(None, None, ("groups", "blk")),
            P(None, None, ("groups", "blk")),
            P(None, ("groups", "blk")),
            P(),
            P(),
            P(("groups", "blk"), None),
            P(("groups", "blk")),
            P(("groups", "blk")),
            P(("groups", "blk")),
        ),
        out_specs=P(None, None, ("groups", "blk")),
        check_vma=False,
    )
```

```python
import functools
import math

import jax
import jax.numpy as jnp
from jax import lax
from jax.experimental import pallas as pl
from jax.experimental.pallas import tpu as pltpu
from jax.sharding import PartitionSpec as P

HARM = 8
PHASES = 512
LAG = 37
ITERS = 4
PSEUDO = 0.2
LANES = 128
SUB = 8
EXACT = lax.Precision.HIGHEST


class Sizes:
    def __init__(self, fields, rows, width, blocks):
        self.fields, self.rows, self.width, self.blocks = fields, rows, width, blocks
        self.groups = width // LANES
        self.cap = 2 * width // blocks
        self.packs = LANES // self.cap
        self.tops = 0
        self.bottoms = self.tops + ITERS * fields * self.groups
        self.visc = self.bottoms + ITERS * fields * self.groups
        self.slot = self.visc + 4 * self.groups
        self.offsets = self.slot + self.groups
        self.weights = self.offsets + SUB
        self.terms = self.weights + SUB
        self.basis = self.terms + 1
        self.table = -(-(self.basis + 1) // SUB) * SUB


def matrix_of(sz, advection, coupling):
    own = [[-PSEUDO * coupling[c, d] for d in range(sz.fields)] for c in range(sz.fields)]
    speed = [PSEUDO * advection[c] for c in range(sz.fields)]
    for c in range(sz.fields):
        own[c][c] = own[c][c] + ((1.0 - 1.5 * PSEUDO) - speed[c])
    return own, speed


def shifted_west(u):
    lane = lax.broadcasted_iota(jnp.int32, u.shape, 1)
    return jnp.where(lane == 0, 0.0, pltpu.roll(u, 1, axis=1))


def shifted_east(u):
    width = u.shape[1]
    lane = lax.broadcasted_iota(jnp.int32, u.shape, 1)
    return jnp.where(lane == width - 1, 0.0, pltpu.roll(u, width - 1, axis=1))


def advance(sz, own, speed, u, visc, column, source):
    out = []
    for c in range(sz.fields):
        west, east = shifted_west(u[c]), shifted_east(u[c])
        new = speed[c] * west + visc * (west + east + column(c) - 4.0 * u[c])
        for d in range(sz.fields):
            new = new + own[c][d] * u[d]
        if source is not None:
            new = new - source(c)
        out.append(new)
    return out


def edge_column(u, ghost, at_low):
    row = lax.broadcasted_iota(jnp.int32, u.shape, 0)
    up, down = pltpu.roll(u, 1, axis=0), pltpu.roll(u, SUB - 1, axis=0)
    if at_low:
        return jnp.where(row == 0, ghost, up) + down
    return up + jnp.where(row == SUB - 1, ghost, down)


def fetch(pairs, sems):
    copies = [pltpu.make_async_copy(src, dst, sems.at[n]) for n, (src, dst) in enumerate(pairs)]
    for copy in copies:
        copy.start()

    def wait():
        for copy in copies:
            copy.wait()

    return wait


def edge_pairs(sz, state, source, viscosity, u_ref, q_ref, v_ref):
    pairs = []
    for n, first in enumerate((0, sz.rows - SUB)):
        here = pl.ds(first, SUB)
        pairs.append((state.at[:, here, :], u_ref.at[n]))
        pairs.append((source.at[:, here, :], q_ref.at[n]))
        pairs.append((viscosity.at[here, :], v_ref.at[n]))
    return pairs


def prepare_kernel(
    sz,
    adv_hbm,
    coup_hbm,
    phase_ref,
    state_hbm,
    source_hbm,
    visc_hbm,
    owner_hbm,
    offset_hbm,
    weight_hbm,
    out_ref,
    adv_ref,
    coup_ref,
    u_both,
    q_both,
    v_both,
    owner_ref,
    offset_ref,
    weight_ref,
    sems,
):
    pairs = edge_pairs(sz, state_hbm, source_hbm, visc_hbm, u_both, q_both, v_both)
    pairs += [(adv_hbm, adv_ref), (coup_hbm, coup_ref)]
    pairs += [(owner_hbm, owner_ref), (offset_hbm, offset_ref), (weight_hbm, weight_ref)]
    fetch(pairs, sems)()
    (low_u, high_u), (low_q, high_q), (low_v, high_v) = [(r.at[0], r.at[1]) for r in (u_both, q_both, v_both)]
    own, speed = matrix_of(sz, adv_ref, coup_ref)

    def put(at, row):
        for g in range(sz.groups):
            out_ref[at + g : at + g + 1, :] = row[:, g * LANES : (g + 1) * LANES]

    out_ref[sz.basis : sz.table, :] = jnp.zeros((sz.table - sz.basis, LANES), jnp.float32)
    for side, (u_ref, q_ref, v_ref, at_low) in enumerate(
        ((high_u, high_q, high_v, False), (low_u, low_q, low_v, True))
    ):
        face = 0 if at_low else SUB - 1
        inner = 1 if at_low else SUB - 2
        base = sz.bottoms if at_low else sz.tops
        visc = PSEUDO * v_ref[...]
        put(sz.visc + (2 * side) * sz.groups, visc[face : face + 1])
        put(sz.visc + (2 * side + 1) * sz.groups, visc[inner : inner + 1])
        u = [u_ref[c] for c in range(sz.fields)]
        q = [PSEUDO * q_ref[c] for c in range(sz.fields)]
        for k in range(ITERS):
            for c in range(sz.fields):
                put(base + (k * sz.fields + c) * sz.groups, u[c][face : face + 1])
            if k < ITERS - 1:
                u = advance(sz, own, speed, u, visc, lambda c: edge_column(u[c], 0.0, at_low), lambda c: q[c])

    owner, offset, weight = owner_ref[...], offset_ref[...], weight_ref[...]
    member = lax.broadcasted_iota(jnp.int32, (sz.blocks, sz.width), 0) == owner
    member = member.astype(jnp.bfloat16)
    before = lax.broadcasted_iota(jnp.int32, (sz.width, sz.width), 0) <= lax.broadcasted_iota(
        jnp.int32, (sz.width, sz.width), 1
    )
    count = jnp.dot(member, before.astype(jnp.bfloat16), preferred_element_type=jnp.float32)
    rank = jnp.sum(count * member.astype(jnp.float32), axis=0, keepdims=True) - 1.0
    rank = rank.astype(jnp.int32)
    slot = owner * sz.cap + rank
    put(sz.slot, slot.astype(jnp.float32))
    place = (lax.broadcasted_iota(jnp.int32, (LANES, sz.width), 0) == slot % LANES).astype(jnp.float32)
    held = lax.broadcasted_iota(jnp.int32, (SUB, sz.width), 0) == slot // LANES
    values = jnp.concatenate(
        [jnp.where(held, offset.astype(jnp.float32), 0.0), jnp.where(held, weight, 0.0)], axis=0
    )
    tables = lax.dot_general(
        values, place, (((1,), (1,)), ((), ())), precision=EXACT, preferred_element_type=jnp.float32
    )
    out_ref[sz.offsets : sz.offsets + 2 * SUB, :] = tables

    order = lax.broadcasted_iota(jnp.int32, (1, LANES), 1)
    harmonic = jnp.where(order > HARM, order - HARM, order).astype(jnp.float32)
    used = order <= 2 * HARM

    def waves(angle):
        product = angle * harmonic
        return jnp.where(order <= HARM, jnp.cos(product), jnp.sin(product))

    phase = phase_ref[0].astype(jnp.float32)
    scale = jnp.where(order == 0, 1.0, 2.0) / sz.blocks
    terms = waves(phase * (2.0 * math.pi / PHASES)) * scale
    basis = waves((phase + LAG) * (2.0 * math.pi / PHASES))
    out_ref[sz.terms : sz.terms + 1, :] = jnp.where(used, terms, 0.0)
    out_ref[sz.basis : sz.basis + 1, :] = jnp.where(used, basis, 0.0)


def interior_kernel(
    sz, adv_hbm, coup_hbm, state_hbm, source_hbm, visc_hbm, out_hbm, adv_ref, coup_ref, u_ref, q_ref, v_ref, work, sems
):
    pairs = [(adv_hbm, adv_ref), (coup_hbm, coup_ref), (state_hbm, u_ref), (source_hbm, q_ref), (visc_hbm, v_ref)]
    fetch(pairs, sems)()
    own, speed = matrix_of(sz, adv_ref, coup_ref)
    tiles = sz.rows // SUB
    row = lax.broadcasted_iota(jnp.int32, (SUB, sz.width), 0)
    for k in range(ITERS):
        src = u_ref if k == 0 else work.at[(k - 1) % 2]
        dst = work.at[k % 2]
        for t in range(tiles):
            here = slice(t * SUB, (t + 1) * SUB)
            u = [src[c, here, :] for c in range(sz.fields)]

            def column(c):
                up, down = pltpu.roll(u[c], 1, axis=0), pltpu.roll(u[c], SUB - 1, axis=0)
                above = src[c, t * SUB - 1 : t * SUB, :] if t > 0 else 0.0
                below = src[c, (t + 1) * SUB : (t + 1) * SUB + 1, :] if t < tiles - 1 else 0.0
                return jnp.where(row == 0, above, up) + jnp.where(row == SUB - 1, below, down)

            new = advance(sz, own, speed, u, PSEUDO * v_ref[here, :], column, lambda c: PSEUDO * q_ref[c, here, :])
            for c in range(sz.fields):
                dst[c, here, :] = new[c]
    fetch([(work.at[(ITERS - 1) % 2], out_hbm)], sems)()


def couple_kernel(
    sz,
    me_ref,
    adv_hbm,
    coup_hbm,
    state_hbm,
    source_hbm,
    visc_hbm,
    even_hbm,
    odd_hbm,
    inside_hbm,
    out_hbm,
    adv_ref,
    coup_ref,
    u_both,
    q_both,
    v_both,
    even_ref,
    odd_ref,
    edge_ref,
    sems,
    slot_offset,
    slot_weight,
    slot_value,
    top_ref,
    next_ref,
    lower_ref,
    bottom_ref,
):
    pairs = [(even_hbm, even_ref), (odd_hbm, odd_ref), (adv_hbm, adv_ref), (coup_hbm, coup_ref)]
    pairs += edge_pairs(sz, state_hbm, source_hbm, visc_hbm, u_both, q_both, v_both)
    ends = [pl.ds(0, SUB), pl.ds(sz.rows - SUB, SUB)]
    pairs += [(inside_hbm.at[:, here, :], edge_ref.at[n]) for n, here in enumerate(ends)]
    fetch(pairs, sems)()
    (low_u, high_u), (low_q, high_q), (low_v, high_v) = [(r.at[0], r.at[1]) for r in (u_both, q_both, v_both)]
    own, speed = matrix_of(sz, adv_ref, coup_ref)
    me = me_ref[0]
    packs, groups, fields = sz.packs, sz.groups, sz.fields
    stride = packs // 2 * sz.table
    lane = lax.broadcasted_iota(jnp.int32, (SUB, LANES), 1)

    def line(b, row):
        ref = (even_ref, odd_ref)[b % 2]
        return ref[pl.ds(b // 2 * sz.table + row, SUB, stride=stride), :]

    def wide(b, row):
        return jnp.concatenate([line(b, row + g) for g in range(groups)], axis=1)

    for m in range(SUB):
        offsets = [line(b, sz.offsets + m) for b in range(packs)]
        weights = [line(b, sz.weights + m) for b in range(packs)]
        for n in range(packs):
            tile_o, tile_w = offsets[n], weights[n]
            for b in range(packs):
                if b != n:
                    mine = lane // sz.cap == b
                    turn = (b - n) * sz.cap % LANES
                    tile_o = jnp.where(mine, pltpu.roll(offsets[b], turn, axis=1), tile_o)
                    tile_w = jnp.where(mine, pltpu.roll(weights[b], turn, axis=1), tile_w)
            o = jnp.bitwise_xor(m * packs + n, me)
            slot_offset[o] = tile_o.astype(jnp.int32)
            slot_weight[o] = tile_w

    slots = [wide(b, sz.slot).astype(jnp.int32) for b in range(packs)]
    takers = [jnp.bitwise_xor(s // sz.cap, me) for s in slots]
    places = [s % sz.cap + b * sz.cap for b, s in enumerate(slots)]
    basis = jnp.concatenate([line(b, sz.basis) for b in range(packs)], axis=0)
    terms = jnp.concatenate([line(b, sz.terms) for b in range(packs)], axis=0)
    kernel = lax.dot_general(
        basis, terms, (((1,), (1,)), ((), ())), precision=EXACT, preferred_element_type=jnp.float32
    )

    def gather(tiles):
        def first_stage(o, carry):
            offset, weight = slot_offset[o], slot_weight[o]
            at, part = offset % LANES, offset // LANES
            for c in range(fields):
                pair = []
                for ref in (top_ref, next_ref):
                    value = None
                    for g in range(groups):
                        source = jnp.broadcast_to(ref[g, o, c : c + 1, :], (SUB, LANES))
                        taken = jnp.take_along_axis(source, at, axis=1)
                        value = taken if value is None else jnp.where(part == g, taken, value)
                    pair.append(value)
                slot_value[o, c] = weight * pair[0] + (1.0 - weight) * pair[1]
            return carry

        lax.fori_loop(0, sz.blocks, first_stage, 0, unroll=min(sz.blocks, 16))
        for b in tiles:
            for g in range(groups):
                cells = slice(g * LANES, (g + 1) * LANES)
                taker, place = takers[b][:, cells], places[b][:, cells]

                def second_stage(o, found):
                    mine = taker == o
                    return tuple(
                        jnp.where(mine, jnp.take_along_axis(slot_value[o, c], place, axis=1), found[c])
                        for c in range(fields)
                    )

                zero = jnp.zeros((SUB, LANES), jnp.float32)
                found = lax.fori_loop(0, sz.blocks, second_stage, (zero,) * fields, unroll=min(sz.blocks, 16))
                for c in range(fields):
                    lower_ref[b, c, :, cells] = found[c]

    def face_step(e, visc, extra):
        return advance(sz, own, speed, e, visc, extra, None)

    visc = {}
    for b in range(packs):
        for n, name in enumerate(("top", "top_in", "bottom", "bottom_in")):
            visc[name, b] = wide(b, sz.visc + n * groups)

    blocks = range(packs)
    outer = {}
    inner = {}
    state = {True: [low_u[c] for c in range(fields)], False: [high_u[c] for c in range(fields)]}
    sources = {True: low_q, False: high_q}
    viscs = {True: PSEUDO * low_v[...], False: PSEUDO * high_v[...]}
    for k in range(ITERS):
        for b in blocks:
            for c in range(fields):
                top = wide(b, sz.tops + (k * fields + c) * groups)
                bottom = wide(b, sz.bottoms + (k * fields + c) * groups)
                if k > 0:
                    top, bottom = top + outer["top", b][c], bottom + outer["bottom", b][c]
                rows = pl.ds(b * SUB + c, SUB, stride=packs * SUB)
                after = pltpu.roll(top, sz.width - 1, axis=1)
                for g in range(groups):
                    cells = slice(g * LANES, (g + 1) * LANES)
                    top_ref.reshape(groups, sz.blocks * SUB, LANES)[g, rows, :] = top[:, cells]
                    next_ref.reshape(groups, sz.blocks * SUB, LANES)[g, rows, :] = after[:, cells]
                bottom_ref[c, b * SUB : (b + 1) * SUB, :] = bottom
        gather(blocks if k < ITERS - 1 else blocks[:1])
        upper = [
            jnp.dot(kernel, bottom_ref[c], precision=EXACT, preferred_element_type=jnp.float32) for c in range(fields)
        ]
        if k < ITERS - 1:
            for b in blocks:
                ghosts = {
                    "top": [upper[c][b * SUB : (b + 1) * SUB] for c in range(fields)],
                    "bottom": [lower_ref[b, c] for c in range(fields)],
                }
                for name, ghost in ghosts.items():
                    v, v_in = visc[name, b], visc[name + "_in", b]
                    if k == 0:
                        outer[name, b] = [v * ghost[c] for c in range(fields)]
                    else:
                        e, e_in = outer[name, b], inner.get((name, b))
                        inner[name, b] = [v_in * e[c] for c in range(fields)]
                        outer[name, b] = face_step(
                            e, v, lambda c: ghost[c] if e_in is None else ghost[c] + e_in[c]
                        )
        for at_low in (True, False):
            u, q = state[at_low], sources[at_low]
            ghost = [(lower_ref[0, c] if at_low else upper[c])[0:1] for c in range(fields)]
            state[at_low] = advance(
                sz, own, speed, u, viscs[at_low], lambda c: edge_column(u[c], ghost[c], at_low), lambda c: PSEUDO * q[c]
            )
    row = lax.broadcasted_iota(jnp.int32, (SUB, sz.width), 0)
    for c in range(fields):
        edge_ref[0, c] = jnp.where(row < SUB // 2, state[True][c], edge_ref[0, c])
        edge_ref[1, c] = jnp.where(row >= SUB // 2, state[False][c], edge_ref[1, c])
    fetch([(edge_ref.at[n], out_hbm.at[:, here, :]) for n, here in enumerate(ends)], sems)()


def spread(table, blocks):
    def swap(piece, mask):
        return lax.ppermute(piece, "blk", [(i, i ^ mask) for i in range(blocks)])

    parts, bit = [table], 4
    while bit < blocks:
        masks = [bit, 2 * bit, 3 * bit] if 2 * bit < blocks else [bit]
        have = jnp.concatenate(parts, axis=0) if len(parts) > 1 else parts[0]
        parts = [have] + [swap(have, mask) for mask in masks]
        bit = bit * (len(masks) + 1)
    twos = [swap(part, 2) for part in parts]

    def single(pieces):
        size = table.shape[0]
        return [piece[n : n + size] for piece in pieces for n in range(0, piece.shape[0], size)]

    even = jnp.concatenate([t for pair in zip(single(parts), single(twos)) for t in pair], axis=0)
    return even, swap(even, 1)


def per_device(
    state_now,
    time_source,
    viscosity,
    advection,
    coupling,
    owner_list,
    owner_offset,
    intersection_weight,
    phase_index,
):
    blocks = lax.axis_size("blk")
    fields, rows, width = state_now.shape
    arrays = (state_now, time_source, viscosity, advection, coupling)
    arrays += tuple(a.reshape(1, width) for a in (owner_list, owner_offset, intersection_weight))
    arrays = [pltpu.with_memory_space_constraint(a, pltpu.HBM) for a in arrays]
    state_now, time_source, viscosity, advection, coupling, owner_list, owner_offset, weight = arrays
    sz = Sizes(fields, rows, width, blocks)
    me = lax.axis_index("blk").astype(jnp.int32).reshape(1)
    smem = pl.BlockSpec(memory_space=pltpu.SMEM)
    vmem = pl.BlockSpec(memory_space=pltpu.VMEM)
    hbm = pl.BlockSpec(memory_space=pltpu.HBM)
    scalars = [pltpu.SMEM((fields,), jnp.float32), pltpu.SMEM((fields, fields), jnp.float32)]
    edges = [
        pltpu.VMEM((2, fields, SUB, width), jnp.float32),
        pltpu.VMEM((2, fields, SUB, width), jnp.float32),
        pltpu.VMEM((2, SUB, width), jnp.float32),
    ]
    half = blocks // 2 * sz.table
    block = jax.ShapeDtypeStruct((fields, rows, width), jnp.float32)
    limit = pltpu.CompilerParams(vmem_limit_bytes=50 * 1024 * 1024)
    table = pl.pallas_call(
        functools.partial(prepare_kernel, sz),
        out_shape=jax.ShapeDtypeStruct((sz.table, LANES), jnp.float32),
        in_specs=[hbm, hbm, smem] + [hbm] * 6,
        out_specs=vmem,
        scratch_shapes=scalars
        + edges
        + [pltpu.VMEM((1, width), kind) for kind in (jnp.int32, jnp.int32, jnp.float32)]
        + [pltpu.SemaphoreType.DMA((11,))],
        compiler_params=limit,
    )(
        advection,
        coupling,
        phase_index,
        state_now,
        time_source,
        viscosity,
        owner_list,
        owner_offset,
        weight,
    )
    even, odd = spread(table, blocks)
    inside = pl.pallas_call(
        functools.partial(interior_kernel, sz),
        out_shape=block,
        in_specs=[hbm] * 5,
        out_specs=hbm,
        scratch_shapes=scalars
        + [
            pltpu.VMEM((fields, rows, width), jnp.float32),
            pltpu.VMEM((fields, rows, width), jnp.float32),
            pltpu.VMEM((rows, width), jnp.float32),
            pltpu.VMEM((2, fields, rows, width), jnp.float32),
            pltpu.SemaphoreType.DMA((5,)),
        ],
        compiler_params=limit,
    )(advection, coupling, state_now, time_source, viscosity)
    return pl.pallas_call(
        functools.partial(couple_kernel, sz),
        out_shape=block,
        in_specs=[smem] + [hbm] * 8,
        out_specs=hbm,
        input_output_aliases={8: 0},
        scratch_shapes=scalars
        + edges
        + [
            pltpu.VMEM((half, LANES), jnp.float32),
            pltpu.VMEM((half, LANES), jnp.float32),
            pltpu.VMEM((2, fields, SUB, width), jnp.float32),
            pltpu.SemaphoreType.DMA((12,)),
            pltpu.VMEM((blocks, SUB, LANES), jnp.int32),
            pltpu.VMEM((blocks, SUB, LANES), jnp.float32),
            pltpu.VMEM((blocks, fields, SUB, LANES), jnp.float32),
            pltpu.VMEM((sz.groups, blocks, SUB, LANES), jnp.float32),
            pltpu.VMEM((sz.groups, blocks, SUB, LANES), jnp.float32),
            pltpu.VMEM((sz.packs, fields, SUB, width), jnp.float32),
            pltpu.VMEM((fields, blocks, width), jnp.float32),
        ],
        compiler_params=limit,
    )(me, advection, coupling, state_now, time_source, viscosity, even, odd, inside)


def solution(mesh):
    return jax.shard_map(
        per_device,
        mesh=mesh,
        in_specs=(
            P(None, None, ("groups", "blk")),
            P(None, None, ("groups", "blk")),
            P(None, ("groups", "blk")),
            P(),
            P(),
            P(("groups", "blk"), None),
            P(("groups", "blk")),
            P(("groups", "blk")),
            P(("groups", "blk")),
        ),
        out_specs=P(None, None, ("groups", "blk")),
        check_vma=False,
    )
```

```python
import functools
import math

import jax
import jax.numpy as jnp
from jax import lax
from jax.experimental import pallas as pl
from jax.experimental.pallas import tpu as pltpu
from jax.sharding import PartitionSpec as P

HARM = 8
PHASES = 512
LAG = 37
ITERS = 4
PSEUDO = 0.2
LANES = 128
SUB = 8
EXACT = lax.Precision.HIGHEST


class Sizes:
    def __init__(self, fields, rows, width, blocks):
        self.fields, self.rows, self.width, self.blocks = fields, rows, width, blocks
        self.groups = width // LANES
        self.cap = 2 * width // blocks
        self.packs = LANES // self.cap
        faces = fields * self.groups
        self.visc = 2 * faces
        self.slot = self.visc + 4 * self.groups
        self.offsets = self.slot + self.groups
        self.weights = self.offsets + SUB
        self.terms = self.weights + SUB
        self.basis = self.terms + 1
        self.first = -(-(self.basis + 1) // SUB) * SUB
        self.rest = -(-2 * (ITERS - 1) * faces // SUB) * SUB

        self.table = self.first + self.rest

    def top(self, k, c):
        return (2 * max(k - 1, 0) * self.fields + c) * self.groups

    def bottom(self, k, c):
        return self.top(k, c) + self.fields * self.groups


def matrix_of(sz, advection, coupling):
    own = [[-PSEUDO * coupling[c, d] for d in range(sz.fields)] for c in range(sz.fields)]
    speed = [PSEUDO * advection[c] for c in range(sz.fields)]
    for c in range(sz.fields):
        own[c][c] = own[c][c] + ((1.0 - 1.5 * PSEUDO) - speed[c])
    return own, speed


def shifted_west(u):
    lane = lax.broadcasted_iota(jnp.int32, u.shape, 1)
    return jnp.where(lane == 0, 0.0, pltpu.roll(u, 1, axis=1))


def shifted_east(u):
    width = u.shape[1]
    lane = lax.broadcasted_iota(jnp.int32, u.shape, 1)
    return jnp.where(lane == width - 1, 0.0, pltpu.roll(u, width - 1, axis=1))


def advance(sz, own, speed, u, visc, column, source):
    out = []
    for c in range(sz.fields):
        west, east = shifted_west(u[c]), shifted_east(u[c])
        new = speed[c] * west + visc * (west + east + column(c) - 4.0 * u[c])
        for d in range(sz.fields):
            new = new + own[c][d] * u[d]
        if source is not None:
            new = new - source(c)
        out.append(new)
    return out


def edge_column(u, ghost, at_low):
    row = lax.broadcasted_iota(jnp.int32, u.shape, 0)
    up, down = pltpu.roll(u, 1, axis=0), pltpu.roll(u, SUB - 1, axis=0)
    if at_low:
        return jnp.where(row == 0, ghost, up) + down
    return up + jnp.where(row == SUB - 1, ghost, down)


def fetch(pairs, sems):
    copies = [pltpu.make_async_copy(src, dst, sems.at[n]) for n, (src, dst) in enumerate(pairs)]
    for copy in copies:
        copy.start()

    def wait():
        for copy in copies:
            copy.wait()

    return wait


def edge_pairs(sz, state, source, viscosity, u_ref, q_ref, v_ref):
    pairs = []
    for n, first in enumerate((0, sz.rows - SUB)):
        here = pl.ds(first, SUB)
        pairs.append((state.at[:, here, :], u_ref.at[n]))
        pairs.append((source.at[:, here, :], q_ref.at[n]))
        pairs.append((viscosity.at[here, :], v_ref.at[n]))
    return pairs


def put(out_ref, at, row):
    for g in range(row.shape[1] // LANES):
        out_ref[at + g : at + g + 1, :] = row[:, g * LANES : (g + 1) * LANES]


def table_kernel(
    sz,
    phase_ref,
    adv_hbm,
    coup_hbm,
    state_hbm,
    source_hbm,
    visc_hbm,
    owner_hbm,
    offset_hbm,
    weight_hbm,
    out_ref,
    adv_ref,
    coup_ref,
    u_both,
    q_both,
    v_both,
    owner_ref,
    offset_ref,
    weight_ref,
    sems,
):
    pairs = [(owner_hbm, owner_ref), (offset_hbm, offset_ref), (weight_hbm, weight_ref)]
    pairs += edge_pairs(sz, state_hbm, source_hbm, visc_hbm, u_both, q_both, v_both)
    pairs += [(adv_hbm, adv_ref), (coup_hbm, coup_ref)]
    arrived = fetch(pairs, sems)
    out_ref[sz.terms : sz.first, :] = jnp.zeros((sz.first - sz.terms, LANES), jnp.float32)
    order = lax.broadcasted_iota(jnp.int32, (1, LANES), 1)
    harmonic = jnp.where(order > HARM, order - HARM, order).astype(jnp.float32)
    used = order <= 2 * HARM

    def waves(angle):
        product = angle * harmonic
        return jnp.where(order <= HARM, jnp.cos(product), jnp.sin(product))

    phase = phase_ref[0].astype(jnp.float32)
    scale = jnp.where(order == 0, 1.0, 2.0) / sz.blocks
    terms = waves(phase * (2.0 * math.pi / PHASES)) * scale
    basis = waves((phase + LAG) * (2.0 * math.pi / PHASES))
    out_ref[sz.terms : sz.terms + 1, :] = jnp.where(used, terms, 0.0)
    out_ref[sz.basis : sz.basis + 1, :] = jnp.where(used, basis, 0.0)
    before = lax.broadcasted_iota(jnp.int32, (sz.width, sz.width), 0) <= lax.broadcasted_iota(
        jnp.int32, (sz.width, sz.width), 1
    )
    before = before.astype(jnp.bfloat16)
    arrived()
    for c in range(sz.fields):
        put(out_ref, sz.top(0, c), u_both[1, c, SUB - 1 : SUB, :])
        put(out_ref, sz.bottom(0, c), u_both[0, c, 0:1, :])
    for n, (end, at) in enumerate(((1, SUB - 1), (1, SUB - 2), (0, 0), (0, 1))):
        put(out_ref, sz.visc + n * sz.groups, PSEUDO * v_both[end, at : at + 1, :])

    owner, offset, weight = owner_ref[...], offset_ref[...], weight_ref[...]
    member = lax.broadcasted_iota(jnp.int32, (sz.blocks, sz.width), 0) == owner
    member = member.astype(jnp.bfloat16)
    count = jnp.dot(member, before, preferred_element_type=jnp.float32)
    rank = jnp.sum(count * member.astype(jnp.float32), axis=0, keepdims=True) - 1.0
    rank = rank.astype(jnp.int32)
    slot = owner * sz.cap + rank
    put(out_ref, sz.slot, slot.astype(jnp.float32))
    place = (lax.broadcasted_iota(jnp.int32, (LANES, sz.width), 0) == slot % LANES).astype(jnp.float32)
    held = lax.broadcasted_iota(jnp.int32, (SUB, sz.width), 0) == slot // LANES
    values = jnp.concatenate(
        [jnp.where(held, offset.astype(jnp.float32), 0.0), jnp.where(held, weight, 0.0)], axis=0
    )
    out_ref[sz.offsets : sz.offsets + 2 * SUB, :] = lax.dot_general(
        values, place, (((1,), (1,)), ((), ())), precision=EXACT, preferred_element_type=jnp.float32
    )

    own, speed = matrix_of(sz, adv_ref, coup_ref)
    for end in range(2):
        at_low = end == 0
        face = 0 if at_low else SUB - 1
        visc = PSEUDO * v_both[end]
        u = [u_both[end, c] for c in range(sz.fields)]
        for k in range(1, ITERS):
            u = advance(
                sz, own, speed, u, visc, lambda c: edge_column(u[c], 0.0, at_low), lambda c: PSEUDO * q_both[end, c]
            )
            for c in range(sz.fields):
                put(out_ref, sz.first + (sz.bottom if at_low else sz.top)(k, c), u[c][face : face + 1])


def interior_kernel(
    sz,
    adv_hbm,
    coup_hbm,
    state_hbm,
    source_hbm,
    visc_hbm,
    after,
    out_hbm,
    passed,
    adv_ref,
    coup_ref,
    u_ref,
    q_ref,
    v_ref,
    work,
    sems,
):
    del after, passed
    pairs = [(adv_hbm, adv_ref), (coup_hbm, coup_ref), (state_hbm, u_ref), (source_hbm, q_ref), (visc_hbm, v_ref)]
    fetch(pairs, sems)()
    own, speed = matrix_of(sz, adv_ref, coup_ref)
    tiles = sz.rows // SUB
    row = lax.broadcasted_iota(jnp.int32, (SUB, sz.width), 0)
    for k in range(ITERS):
        src = u_ref if k == 0 else work.at[(k - 1) % 2]
        dst = work.at[k % 2]
        for t in range(tiles):
            here = slice(t * SUB, (t + 1) * SUB)
            u = [src[c, here, :] for c in range(sz.fields)]

            def column(c):
                up, down = pltpu.roll(u[c], 1, axis=0), pltpu.roll(u[c], SUB - 1, axis=0)
                above = src[c, t * SUB - 1 : t * SUB, :] if t > 0 else 0.0
                below = src[c, (t + 1) * SUB : (t + 1) * SUB + 1, :] if t < tiles - 1 else 0.0
                return jnp.where(row == 0, above, up) + jnp.where(row == SUB - 1, below, down)

            new = advance(sz, own, speed, u, PSEUDO * v_ref[here, :], column, lambda c: PSEUDO * q_ref[c, here, :])
            for c in range(sz.fields):
                dst[c, here, :] = new[c]
    fetch([(work.at[(ITERS - 1) % 2], out_hbm)], sems)()


def faces_of(sz, even_ref, odd_ref, base):
    def line(b, row):
        ref = (even_ref, odd_ref)[b % 2]
        return ref[pl.ds(b // 2 * sz.table + base + row, SUB, stride=sz.packs // 2 * sz.table), :]

    def wide(b, row):
        return jnp.concatenate([line(b, row + g) for g in range(sz.groups)], axis=1)

    return line, wide


def keep_faces(sz, b, c, top, bottom, top_ref, next_ref, bottom_ref):
    rows = pl.ds(b * SUB + c, SUB, stride=sz.packs * SUB)
    after = pltpu.roll(top, sz.width - 1, axis=1)
    for g in range(sz.groups):
        cells = slice(g * LANES, (g + 1) * LANES)
        top_ref.reshape(sz.groups, sz.blocks * SUB, LANES)[g, rows, :] = top[:, cells]
        next_ref.reshape(sz.groups, sz.blocks * SUB, LANES)[g, rows, :] = after[:, cells]
    bottom_ref[c, b * SUB : (b + 1) * SUB, :] = bottom


def gather(sz, slot_offset, slot_weight, slot_value, top_ref, next_ref, taker_ref, place_ref, lower_ref):
    fields, groups = sz.fields, sz.groups
    unroll = min(sz.blocks, 16)

    def first_stage(o, carry):
        offset, weight = slot_offset[o], slot_weight[o]
        at, part = offset % LANES, offset // LANES
        for c in range(fields):
            pair = []
            for ref in (top_ref, next_ref):
                value = None
                for g in range(groups):
                    source = jnp.broadcast_to(ref[g, o, c : c + 1, :], (SUB, LANES))
                    taken = jnp.take_along_axis(source, at, axis=1)
                    value = taken if value is None else jnp.where(part == g, taken, value)
                pair.append(value)
            slot_value[o, c] = weight * pair[0] + (1.0 - weight) * pair[1]
        return carry

    lax.fori_loop(0, sz.blocks, first_stage, 0, unroll=unroll)
    for b in range(sz.packs):
        for g in range(groups):
            cells = slice(g * LANES, (g + 1) * LANES)
            taker, place = taker_ref[b, :, cells], place_ref[b, :, cells]

            def second_stage(o, found):
                mine = taker == o
                return tuple(
                    jnp.where(mine, jnp.take_along_axis(slot_value[o, c], place, axis=1), found[c])
                    for c in range(fields)
                )

            zero = jnp.zeros((SUB, LANES), jnp.float32)
            found = lax.fori_loop(0, sz.blocks, second_stage, (zero,) * fields, unroll=unroll)
            for c in range(fields):
                lower_ref[b, c, :, cells] = found[c]


def gather_own(sz, own_offset, own_weight, top_ref, next_ref, taker, place):
    fields, groups, packs = sz.fields, sz.groups, sz.packs
    lane = lax.broadcasted_iota(jnp.int32, (SUB, LANES), 1)
    at, part = own_offset % LANES, own_offset // LANES

    def stacked(row):
        parts = [row[:, g * LANES : (g + 1) * LANES] for g in range(groups)]
        return jnp.concatenate(parts + [parts[0]] * (SUB - groups), axis=0)

    taker, place = stacked(taker), stacked(place)
    place = place + taker % packs * sz.cap
    ghost = []
    for c in range(fields):
        pair = []
        for ref in (top_ref, next_ref):
            value = jnp.zeros((SUB, LANES), jnp.float32)
            for b in range(packs):
                rows = pl.ds(b * SUB + c, SUB, stride=packs * SUB)
                for g in range(groups):
                    source = ref.reshape(groups, sz.blocks * SUB, LANES)[g, rows, :]
                    here = (part == g) & (lane // sz.cap == b)
                    value = jnp.where(here, jnp.take_along_axis(source, at, axis=1), value)
            pair.append(value)
        held = own_weight * pair[0] + (1.0 - own_weight) * pair[1]
        found = jnp.zeros((SUB, LANES), jnp.float32)
        for m in range(SUB):
            source = jnp.broadcast_to(held[m : m + 1], (SUB, LANES))
            found = jnp.where(taker // packs == m, jnp.take_along_axis(source, place, axis=1), found)
        ghost.append(jnp.concatenate([found[g : g + 1] for g in range(groups)], axis=1))
    return ghost


def mixed(kernel, bottom_ref, fields):
    return [jnp.dot(kernel, bottom_ref[c], precision=EXACT, preferred_element_type=jnp.float32) for c in range(fields)]


def couple_first(
    sz,
    me,
    even_ref,
    odd_ref,
    slot_offset,
    slot_weight,
    own_offset,
    own_weight,
    taker_ref,
    place_ref,
    kernel_ref,
    visc_ref,
    outer_ref,
    ghost_ref,
    slot_value,
    top_ref,
    next_ref,
    lower_ref,
    bottom_ref,
):
    packs, groups, fields = sz.packs, sz.groups, sz.fields
    lane = lax.broadcasted_iota(jnp.int32, (SUB, LANES), 1)
    line, wide = faces_of(sz, even_ref, odd_ref, 0)
    for b in range(packs):
        for c in range(fields):
            top, bottom = wide(b, sz.top(0, c)), wide(b, sz.bottom(0, c))
            keep_faces(sz, b, c, top, bottom, top_ref, next_ref, bottom_ref)

    for m in range(SUB):
        offsets = [line(b, sz.offsets + m) for b in range(packs)]
        weights = [line(b, sz.weights + m) for b in range(packs)]
        for n in range(packs):
            tile_o, tile_w = offsets[n], weights[n]
            for b in range(packs):
                if b != n:
                    mine = lane // sz.cap == b
                    turn = (b - n) * sz.cap % LANES
                    tile_o = jnp.where(mine, pltpu.roll(offsets[b], turn, axis=1), tile_o)
                    tile_w = jnp.where(mine, pltpu.roll(weights[b], turn, axis=1), tile_w)
            o = jnp.bitwise_xor(m * packs + n, me)
            slot_offset[o] = tile_o.astype(jnp.int32)
            slot_weight[o] = tile_w
    for b in range(packs):
        slots = wide(b, sz.slot).astype(jnp.int32)
        taker_ref[b] = jnp.bitwise_xor(slots // sz.cap, me)
        place_ref[b] = slots % sz.cap + b * sz.cap
        for n in range(4):
            visc_ref[n, b] = wide(b, sz.visc + n * groups)
    basis = jnp.concatenate([line(b, sz.basis) for b in range(packs)], axis=0)
    terms = jnp.concatenate([line(b, sz.terms) for b in range(packs)], axis=0)
    kernel = lax.dot_general(
        basis, terms, (((1,), (1,)), ((), ())), precision=EXACT, preferred_element_type=jnp.float32
    )
    kernel_ref[...] = kernel

    sublane = lax.broadcasted_iota(jnp.int32, (SUB, LANES), 0)
    for ref, out in ((slot_offset, own_offset), (slot_weight, own_weight)):
        tile = jnp.zeros((SUB, LANES), out.dtype)
        for o in range(sz.blocks):
            here = (sublane == o // packs) & (lane // sz.cap == o % packs)
            turn = o % packs * sz.cap
            line_o = jnp.broadcast_to(ref[o, 0:1, :], (SUB, LANES))
            tile = jnp.where(here, pltpu.roll(line_o, turn, axis=1) if turn else line_o, tile)
        out[...] = tile

    upper = mixed(kernel, bottom_ref, fields)
    gather(sz, slot_offset, slot_weight, slot_value, top_ref, next_ref, taker_ref, place_ref, lower_ref)
    for c in range(fields):
        ghost_ref[0, c] = lower_ref[0, c]
        ghost_ref[1, c] = upper[c][0:SUB]
        for b in range(packs):
            outer_ref[0, b, c] = visc_ref[0, b] * upper[c][b * SUB : (b + 1) * SUB]
            outer_ref[1, b, c] = visc_ref[2, b] * lower_ref[b, c]


def couple_kernel(sz, me_ref, adv_hbm, coup_hbm, visc_hbm, even_ref, odd_ref, inside_hbm, out_hbm, *scratch):
    adv_ref, coup_ref, ends_ref, edge_ref, sems = scratch[:5]
    carried, work = scratch[5:-5], scratch[-5:]
    slot_offset, slot_weight, own_offset, own_weight, taker_ref, place_ref, kernel_ref, visc_ref, outer_ref, ghost_ref = carried
    slot_value, top_ref, next_ref, lower_ref, bottom_ref = work
    ends = [pl.ds(0, SUB), pl.ds(sz.rows - SUB, SUB)]
    pairs = [(adv_hbm, adv_ref), (coup_hbm, coup_ref)]
    pairs += [(visc_hbm.at[here, :], ends_ref.at[n]) for n, here in enumerate(ends)]
    pairs += [(inside_hbm.at[:, here, :], edge_ref.at[n]) for n, here in enumerate(ends)]
    arrived = fetch(pairs, sems)
    couple_first(sz, me_ref[0], even_ref, odd_ref, *carried, *work)
    packs, fields = sz.packs, sz.fields
    _, wide = faces_of(sz, even_ref, odd_ref, sz.first)
    kernel = kernel_ref[...]
    outer = {(n, b): [outer_ref[n, b, c] for c in range(fields)] for n in range(2) for b in range(packs)}
    inner = {}

    half = SUB // 2
    row = lax.broadcasted_iota(jnp.int32, (SUB, sz.width), 0)

    def ghosts_only(lower, upper):
        return [jnp.where(row == 0, lower[c], jnp.where(row == SUB - 1, upper[c], 0.0)) for c in range(fields)]

    for k in range(1, ITERS):
        for b in range(packs):
            for c in range(fields):
                top = wide(b, sz.top(k, c)) + outer[0, b][c]
                bottom = wide(b, sz.bottom(k, c)) + outer[1, b][c]
                keep_faces(sz, b, c, top, bottom, top_ref, next_ref, bottom_ref)
        if k == ITERS - 1:
            upper = mixed(kernel[:SUB], bottom_ref, fields)
            taker, place = taker_ref[0, 0:1, :], place_ref[0, 0:1, :]
            lower = gather_own(sz, own_offset[...], own_weight[...], top_ref, next_ref, taker, place)
        else:
            upper = mixed(kernel, bottom_ref, fields)
            gather(sz, slot_offset, slot_weight, slot_value, top_ref, next_ref, taker_ref, place_ref, lower_ref)
            lower = [lower_ref[0, c, 0:1, :] for c in range(fields)]
            if k == 1:
                arrived()
                own, speed = matrix_of(sz, adv_ref, coup_ref)
            for n in range(2):
                for b in range(packs):
                    e, e_in = outer[n, b], inner.get((n, b))
                    inner[n, b] = [visc_ref[2 * n + 1, b] * e[c] for c in range(fields)]

                    def column(c):
                        next_to = upper[c][b * SUB : (b + 1) * SUB] if n == 0 else lower_ref[b, c]
                        return next_to if e_in is None else next_to + e_in[c]

                    outer[n, b] = advance(sz, own, speed, e, visc_ref[2 * n, b], column, None)
        if k == 1:
            visc = PSEUDO * jnp.where(row < half, ends_ref[0], ends_ref[1])
            firsts = [[ghost_ref[n, c, 0:1, :] for c in range(fields)] for n in range(2)]
            forced = [visc * g for g in ghosts_only(*firsts)]
        ghost = ghosts_only(lower, [upper[c][0:1] for c in range(fields)])

        def around(c):
            up = jnp.where((row == 0) | (row == half), 0.0, pltpu.roll(forced[c], 1, axis=0))
            down = jnp.where((row == SUB - 1) | (row == half - 1), 0.0, pltpu.roll(forced[c], SUB - 1, axis=0))
            return up + down + ghost[c]

        forced = advance(sz, own, speed, forced, visc, around, None)
    for c in range(fields):
        edge_ref[0, c] = edge_ref[0, c] + jnp.where(row < half, forced[c], 0.0)
        edge_ref[1, c] = edge_ref[1, c] + jnp.where(row >= half, forced[c], 0.0)
    fetch([(edge_ref.at[n], out_hbm.at[:, here, :]) for n, here in enumerate(ends)], sems)()


def spread(table, blocks, between):
    def swap(piece, mask):
        return lax.ppermute(piece, "blk", [(i, i ^ mask) for i in range(blocks)])

    parts, bit = [table], 4
    while bit < blocks:
        masks = [bit, 2 * bit, 3 * bit] if 2 * bit < blocks else [bit]
        have = jnp.concatenate(parts, axis=0) if len(parts) > 1 else parts[0]
        parts = [have] + [swap(have, mask) for mask in masks]
        bit = bit * (len(masks) + 1)
    parts[1] = between(parts[1])
    twos = [swap(part, 2) for part in parts]
    even = jnp.concatenate([t for pair in zip(parts, twos) for t in pair], axis=0)
    return even, swap(even, 1)


def per_device(
    state_now,
    time_source,
    viscosity,
    advection,
    coupling,
    owner_list,
    owner_offset,
    intersection_weight,
    phase_index,
):
    blocks = lax.axis_size("blk")
    fields, rows, width = state_now.shape
    arrays = (state_now, time_source, viscosity, advection, coupling)
    arrays += tuple(a.reshape(1, width) for a in (owner_list, owner_offset, intersection_weight))
    arrays = [pltpu.with_memory_space_constraint(a, pltpu.HBM) for a in arrays]
    state_now, time_source, viscosity, advection, coupling, owner_list, owner_offset, weight = arrays
    sz = Sizes(fields, rows, width, blocks)
    me = lax.axis_index("blk").astype(jnp.int32).reshape(1)
    smem = pl.BlockSpec(memory_space=pltpu.SMEM)
    vmem = pl.BlockSpec(memory_space=pltpu.VMEM)
    hbm = pl.BlockSpec(memory_space=pltpu.HBM)
    anywhere = pl.BlockSpec(memory_space=pl.ANY)
    f32, i32 = jnp.float32, jnp.int32
    scalars = [pltpu.SMEM((fields,), f32), pltpu.SMEM((fields, fields), f32)]
    block = jax.ShapeDtypeStruct((fields, rows, width), f32)
    limit = pltpu.CompilerParams(vmem_limit_bytes=50 * 1024 * 1024)
    two_ends = pltpu.VMEM((2, fields, SUB, width), f32)
    visc_ends = pltpu.VMEM((2, SUB, width), f32)
    table = pl.pallas_call(
        functools.partial(table_kernel, sz),
        out_shape=jax.ShapeDtypeStruct((sz.table, LANES), f32),
        in_specs=[smem] + [hbm] * 8,
        out_specs=vmem,
        scratch_shapes=scalars
        + [two_ends, two_ends, visc_ends]
        + [pltpu.VMEM((1, width), kind) for kind in (i32, i32, f32)]
        + [pltpu.SemaphoreType.DMA((11,))],
        compiler_params=limit,
    )(phase_index, advection, coupling, state_now, time_source, viscosity, owner_list, owner_offset, weight)
    insides = []

    def interior(piece):
        inside, piece = pl.pallas_call(
            functools.partial(interior_kernel, sz),
            out_shape=[block, jax.ShapeDtypeStruct(piece.shape, piece.dtype)],
            in_specs=[hbm] * 5 + [anywhere],
            out_specs=[hbm, anywhere],
            input_output_aliases={5: 1},
            scratch_shapes=scalars
            + [
                pltpu.VMEM((fields, rows, width), f32),
                pltpu.VMEM((fields, rows, width), f32),
                pltpu.VMEM((rows, width), f32),
                pltpu.VMEM((2, fields, rows, width), f32),
                pltpu.SemaphoreType.DMA((5,)),
            ],
            compiler_params=limit,
        )(advection, coupling, state_now, time_source, viscosity, piece)
        insides.append(inside)
        return piece

    even, odd = spread(table, blocks, interior)
    work = [
        pltpu.VMEM((blocks, fields, SUB, LANES), f32),
        pltpu.VMEM((sz.groups, blocks, SUB, LANES), f32),
        pltpu.VMEM((sz.groups, blocks, SUB, LANES), f32),
        pltpu.VMEM((sz.packs, fields, SUB, width), f32),
        pltpu.VMEM((fields, blocks, width), f32),
    ]
    carried = [
        pltpu.VMEM((blocks, SUB, LANES), i32),
        pltpu.VMEM((blocks, SUB, LANES), f32),
        pltpu.VMEM((SUB, LANES), i32),
        pltpu.VMEM((SUB, LANES), f32),
        pltpu.VMEM((sz.packs, SUB, width), i32),
        pltpu.VMEM((sz.packs, SUB, width), i32),
        pltpu.VMEM((blocks, blocks), f32),
        pltpu.VMEM((4, sz.packs, SUB, width), f32),
        pltpu.VMEM((2, sz.packs, fields, SUB, width), f32),
        pltpu.VMEM((2, fields, SUB, width), f32),
    ]
    return pl.pallas_call(
        functools.partial(couple_kernel, sz),
        out_shape=block,
        in_specs=[smem] + [hbm] * 3 + [vmem] * 2 + [hbm],
        out_specs=hbm,
        input_output_aliases={6: 0},
        scratch_shapes=scalars + [visc_ends, two_ends, pltpu.SemaphoreType.DMA((6,))] + carried + work,
        compiler_params=limit,
    )(me, advection, coupling, viscosity, even, odd, insides[0])


def solution(mesh):
    return jax.shard_map(
        per_device,
        mesh=mesh,
        in_specs=(
            P(None, None, ("groups", "blk")),
            P(None, None, ("groups", "blk")),
            P(None, ("groups", "blk")),
            P(),
            P(),
            P(("groups", "blk"), None),
            P(("groups", "blk")),
            P(("groups", "blk")),
            P(("groups", "blk")),
        ),
        out_specs=P(None, None, ("groups", "blk")),
        check_vma=False,
    )
```

```python
import functools
import math

import jax
import jax.numpy as jnp
from jax import lax
from jax.experimental import pallas as pl
from jax.experimental.pallas import tpu as pltpu
from jax.sharding import PartitionSpec as P

HARM = 8
PHASES = 512
LAG = 37
ITERS = 4
PSEUDO = 0.2
LANES = 128
SUB = 8
EXACT = lax.Precision.HIGHEST


class Sizes:
    def __init__(self, fields, rows, width, blocks):
        self.fields, self.rows, self.width, self.blocks = fields, rows, width, blocks
        self.groups = width // LANES
        self.cap = 2 * width // blocks
        self.packs = LANES // self.cap
        faces = fields * self.groups
        self.visc = 2 * faces
        self.slot = self.visc + 4 * self.groups
        self.offsets = self.slot + self.groups
        self.weights = self.offsets + SUB
        self.terms = self.weights + SUB
        self.basis = self.terms + 1
        self.first = -(-(self.basis + 1) // SUB) * SUB
        self.rest = -(-2 * (ITERS - 1) * faces // SUB) * SUB

        self.table = self.first + self.rest

    def top(self, k, c):
        return (2 * max(k - 1, 0) * self.fields + c) * self.groups

    def bottom(self, k, c):
        return self.top(k, c) + self.fields * self.groups


def matrix_of(sz, advection, coupling):
    own = [[-PSEUDO * coupling[c, d] for d in range(sz.fields)] for c in range(sz.fields)]
    speed = [PSEUDO * advection[c] for c in range(sz.fields)]
    for c in range(sz.fields):
        own[c][c] = own[c][c] + ((1.0 - 1.5 * PSEUDO) - speed[c])
    return own, speed


def shifted_west(u):
    lane = lax.broadcasted_iota(jnp.int32, u.shape, 1)
    return jnp.where(lane == 0, 0.0, pltpu.roll(u, 1, axis=1))


def shifted_east(u):
    width = u.shape[1]
    lane = lax.broadcasted_iota(jnp.int32, u.shape, 1)
    return jnp.where(lane == width - 1, 0.0, pltpu.roll(u, width - 1, axis=1))


def advance(sz, own, speed, u, visc, column, source):
    out = []
    for c in range(sz.fields):
        west, east = shifted_west(u[c]), shifted_east(u[c])
        new = speed[c] * west + visc * (west + east + column(c) - 4.0 * u[c])
        for d in range(sz.fields):
            new = new + own[c][d] * u[d]
        if source is not None:
            new = new - source(c)
        out.append(new)
    return out


def inside_column(u):
    row = lax.broadcasted_iota(jnp.int32, u.shape, 0)
    half = SUB // 2
    up = jnp.where((row == 0) | (row == half), 0.0, pltpu.roll(u, 1, axis=0))
    down = jnp.where((row == SUB - 1) | (row == half - 1), 0.0, pltpu.roll(u, SUB - 1, axis=0))
    return up + down


def in_parts(x):
    high = x.astype(jnp.bfloat16)
    rest = x - high.astype(jnp.float32)
    middle = rest.astype(jnp.bfloat16)
    low = (rest - middle.astype(jnp.float32)).astype(jnp.bfloat16)
    return high, middle, low


def fetch(pairs, sems):
    copies = [pltpu.make_async_copy(src, dst, sems.at[n]) for n, (src, dst) in enumerate(pairs)]
    for copy in copies:
        copy.start()

    def wait():
        for copy in copies:
            copy.wait()

    return wait


def edge_pairs(sz, state, source, viscosity, u_ref, q_ref, v_ref):
    pairs = []
    for n, first in enumerate((0, sz.rows - SUB)):
        here = pl.ds(first, SUB)
        pairs.append((state.at[:, here, :], u_ref.at[n]))
        pairs.append((source.at[:, here, :], q_ref.at[n]))
        pairs.append((viscosity.at[here, :], v_ref.at[n]))
    return pairs


def put(out_ref, at, row):
    for g in range(row.shape[1] // LANES):
        out_ref[at + g : at + g + 1, :] = row[:, g * LANES : (g + 1) * LANES]


def table_kernel(
    sz,
    phase_ref,
    adv_hbm,
    coup_hbm,
    state_hbm,
    source_hbm,
    visc_hbm,
    owner_hbm,
    offset_hbm,
    weight_hbm,
    out_ref,
    adv_ref,
    coup_ref,
    u_both,
    q_both,
    v_both,
    owner_ref,
    offset_ref,
    weight_ref,
    sems,
):
    pairs = [(owner_hbm, owner_ref), (offset_hbm, offset_ref), (weight_hbm, weight_ref)]
    lists_in = fetch(pairs, sems.at[pl.ds(0, 3)])
    pairs = edge_pairs(sz, state_hbm, source_hbm, visc_hbm, u_both, q_both, v_both)
    pairs += [(adv_hbm, adv_ref), (coup_hbm, coup_ref)]
    edges_in = fetch(pairs, sems.at[pl.ds(3, 8)])
    out_ref[sz.terms : sz.first, :] = jnp.zeros((sz.first - sz.terms, LANES), jnp.float32)
    order = lax.broadcasted_iota(jnp.int32, (1, LANES), 1)
    harmonic = jnp.where(order > HARM, order - HARM, order).astype(jnp.float32)
    used = order <= 2 * HARM

    def waves(angle):
        product = angle * harmonic
        return jnp.where(order <= HARM, jnp.cos(product), jnp.sin(product))

    phase = phase_ref[0].astype(jnp.float32)
    scale = jnp.where(order == 0, 1.0, 2.0) / sz.blocks
    terms = waves(phase * (2.0 * math.pi / PHASES)) * scale
    basis = waves((phase + LAG) * (2.0 * math.pi / PHASES))
    out_ref[sz.terms : sz.terms + 1, :] = jnp.where(used, terms, 0.0)
    out_ref[sz.basis : sz.basis + 1, :] = jnp.where(used, basis, 0.0)
    before = lax.broadcasted_iota(jnp.int32, (sz.width, sz.width), 0) <= lax.broadcasted_iota(
        jnp.int32, (sz.width, sz.width), 1
    )
    before = before.astype(jnp.bfloat16)
    lists_in()
    owner, offset, weight = owner_ref[...], offset_ref[...], weight_ref[...]
    member = lax.broadcasted_iota(jnp.int32, (sz.blocks, sz.width), 0) == owner
    member = member.astype(jnp.bfloat16)
    count = jnp.dot(member, before, preferred_element_type=jnp.float32)
    rank = jnp.sum(count * member.astype(jnp.float32), axis=0, keepdims=True) - 1.0
    rank = rank.astype(jnp.int32)
    slot = owner * sz.cap + rank
    put(out_ref, sz.slot, slot.astype(jnp.float32))
    place = (lax.broadcasted_iota(jnp.int32, (LANES, sz.width), 0) == slot % LANES).astype(jnp.bfloat16)
    held = lax.broadcasted_iota(jnp.int32, (SUB, sz.width), 0) == slot // LANES
    values = jnp.concatenate(
        [jnp.where(held, offset.astype(jnp.float32), 0.0), jnp.where(held, weight, 0.0)], axis=0
    )
    parts = jnp.concatenate(in_parts(values), axis=0)
    high, middle, low = jnp.split(
        lax.dot_general(parts, place, (((1,), (1,)), ((), ())), preferred_element_type=jnp.float32), 3, axis=0
    )
    out_ref[sz.offsets : sz.offsets + 2 * SUB, :] = high + (middle + low)

    edges_in()
    for c in range(sz.fields):
        put(out_ref, sz.top(0, c), u_both[1, c, SUB - 1 : SUB, :])
        put(out_ref, sz.bottom(0, c), u_both[0, c, 0:1, :])
    for n, (end, at) in enumerate(((1, SUB - 1), (1, SUB - 2), (0, 0), (0, 1))):
        put(out_ref, sz.visc + n * sz.groups, PSEUDO * v_both[end, at : at + 1, :])
    own, speed = matrix_of(sz, adv_ref, coup_ref)
    half = SUB // 2
    row = lax.broadcasted_iota(jnp.int32, (SUB, sz.width), 0)

    def both(low, high):
        return jnp.where(row < half, low, high)

    visc = PSEUDO * both(v_both[0], v_both[1])
    source = [PSEUDO * both(q_both[0, c], q_both[1, c]) for c in range(sz.fields)]
    u = [both(u_both[0, c], u_both[1, c]) for c in range(sz.fields)]
    for k in range(1, ITERS):
        u = advance(sz, own, speed, u, visc, lambda c: inside_column(u[c]), lambda c: source[c])
        for c in range(sz.fields):
            put(out_ref, sz.first + sz.top(k, c), u[c][SUB - 1 : SUB])
            put(out_ref, sz.first + sz.bottom(k, c), u[c][0:1])


def interior_kernel(
    sz,
    adv_hbm,
    coup_hbm,
    state_hbm,
    source_hbm,
    visc_hbm,
    after,
    out_hbm,
    passed,
    adv_ref,
    coup_ref,
    u_ref,
    q_ref,
    v_ref,
    work,
    sems,
):
    del after, passed
    pairs = [(adv_hbm, adv_ref), (coup_hbm, coup_ref), (state_hbm, u_ref), (source_hbm, q_ref), (visc_hbm, v_ref)]
    fetch(pairs, sems)()
    own, speed = matrix_of(sz, adv_ref, coup_ref)
    tiles = sz.rows // SUB
    row = lax.broadcasted_iota(jnp.int32, (SUB, sz.width), 0)
    for k in range(ITERS):
        src = u_ref if k == 0 else work.at[(k - 1) % 2]
        dst = work.at[k % 2]
        for t in range(tiles):
            here = slice(t * SUB, (t + 1) * SUB)
            u = [src[c, here, :] for c in range(sz.fields)]

            def column(c):
                up, down = pltpu.roll(u[c], 1, axis=0), pltpu.roll(u[c], SUB - 1, axis=0)
                above = src[c, t * SUB - 1 : t * SUB, :] if t > 0 else 0.0
                below = src[c, (t + 1) * SUB : (t + 1) * SUB + 1, :] if t < tiles - 1 else 0.0
                return jnp.where(row == 0, above, up) + jnp.where(row == SUB - 1, below, down)

            new = advance(sz, own, speed, u, PSEUDO * v_ref[here, :], column, lambda c: PSEUDO * q_ref[c, here, :])
            for c in range(sz.fields):
                dst[c, here, :] = new[c]
    fetch([(work.at[(ITERS - 1) % 2], out_hbm)], sems)()


def faces_of(sz, even_ref, odd_ref, base):
    def line(b, row):
        ref = (even_ref, odd_ref)[b % 2]
        return ref[pl.ds(b // 2 * sz.table + base + row, SUB, stride=sz.packs // 2 * sz.table), :]

    def wide(b, row):
        return jnp.concatenate([line(b, row + g) for g in range(sz.groups)], axis=1)

    return line, wide


def keep_faces(sz, b, c, top, bottom, top_ref, next_ref, bottom_ref):
    after = pltpu.roll(top, sz.width - 1, axis=1)
    for g in range(sz.groups):
        cells = slice(g * LANES, (g + 1) * LANES)
        top_ref[b, g, c] = top[:, cells]
        next_ref[b, g, c] = after[:, cells]
    bottom_ref[c, b * SUB : (b + 1) * SUB, :] = bottom


def gather(sz, slot_offset, slot_weight, slot_value, top_ref, next_ref, taker_ref, place_ref, lower_ref):
    fields, groups = sz.fields, sz.groups
    unroll = min(sz.blocks, 16)

    def first_stage(sub, b, carry):
        o = sz.packs * sub + b
        offset, weight = slot_offset[o], slot_weight[o]
        at, part = offset % LANES, offset // LANES
        for c in range(fields):
            pair = []
            for ref in (top_ref, next_ref):
                value = None
                for g in range(groups):
                    source = jnp.broadcast_to(ref[b, g, c, sub : sub + 1, :], (SUB, LANES))
                    taken = jnp.take_along_axis(source, at, axis=1)
                    value = taken if value is None else jnp.where(part == g, taken, value)
                pair.append(value)
            slot_value[o, c] = weight * pair[0] + (1.0 - weight) * pair[1]
        return carry

    for sub in range(SUB):
        lax.fori_loop(0, sz.packs, functools.partial(first_stage, sub), 0, unroll=min(sz.packs, 2))
    for b in range(sz.packs):
        for g in range(groups):
            cells = slice(g * LANES, (g + 1) * LANES)
            taker, place = taker_ref[b, :, cells], place_ref[b, :, cells]

            def second_stage(o, found):
                mine = taker == o
                return tuple(
                    jnp.where(mine, jnp.take_along_axis(slot_value[o, c], place, axis=1), found[c])
                    for c in range(fields)
                )

            zero = jnp.zeros((SUB, LANES), jnp.float32)
            found = lax.fori_loop(0, sz.blocks, second_stage, (zero,) * fields, unroll=unroll)
            for c in range(fields):
                lower_ref[b, c, :, cells] = found[c]


def gather_own(sz, own_offset, own_weight, top_ref, next_ref, taker, place):
    fields, groups, packs = sz.fields, sz.groups, sz.packs
    lane = lax.broadcasted_iota(jnp.int32, (SUB, LANES), 1)
    at, part = own_offset % LANES, own_offset // LANES

    def stacked(row):
        parts = [row[:, g * LANES : (g + 1) * LANES] for g in range(groups)]
        return jnp.concatenate(parts + [parts[0]] * (SUB - groups), axis=0)

    taker, place = stacked(taker), stacked(place)
    place = place + taker % packs * sz.cap
    ghost = []
    for c in range(fields):
        pair = []
        for ref in (top_ref, next_ref):
            value = jnp.zeros((SUB, LANES), jnp.float32)
            for b in range(packs):
                for g in range(groups):
                    source = ref[b, g, c]
                    here = (part == g) & (lane // sz.cap == b)
                    value = jnp.where(here, jnp.take_along_axis(source, at, axis=1), value)
            pair.append(value)
        held = own_weight * pair[0] + (1.0 - own_weight) * pair[1]
        found = jnp.zeros((SUB, LANES), jnp.float32)
        for m in range(SUB):
            source = jnp.broadcast_to(held[m : m + 1], (SUB, LANES))
            found = jnp.where(taker // packs == m, jnp.take_along_axis(source, place, axis=1), found)
        ghost.append(jnp.concatenate([found[g : g + 1] for g in range(groups)], axis=1))
    return ghost


def mixed(kernel, bottom_ref, fields):
    high, middle, low = in_parts(kernel)
    left = jnp.concatenate([high, high, high, middle, middle, low], axis=1)
    out = []
    for c in range(fields):
        high, middle, low = in_parts(bottom_ref[c])
        right = jnp.concatenate([high, middle, low, high, middle, high], axis=0)
        out.append(jnp.dot(left, right, preferred_element_type=jnp.float32))
    return out


def couple_first(
    sz,
    me,
    even_ref,
    odd_ref,
    slot_offset,
    slot_weight,
    own_offset,
    own_weight,
    taker_ref,
    place_ref,
    kernel_ref,
    visc_ref,
    outer_ref,
    ghost_ref,
    slot_value,
    top_ref,
    next_ref,
    lower_ref,
    bottom_ref,
):
    packs, groups, fields = sz.packs, sz.groups, sz.fields
    lane = lax.broadcasted_iota(jnp.int32, (SUB, LANES), 1)
    line, wide = faces_of(sz, even_ref, odd_ref, 0)
    for b in range(packs):
        for c in range(fields):
            top, bottom = wide(b, sz.top(0, c)), wide(b, sz.bottom(0, c))
            keep_faces(sz, b, c, top, bottom, top_ref, next_ref, bottom_ref)

    for m in range(SUB):
        offsets = [line(b, sz.offsets + m) for b in range(packs)]
        weights = [line(b, sz.weights + m) for b in range(packs)]
        for n in range(packs):
            tile_o, tile_w = offsets[n], weights[n]
            for b in range(packs):
                if b != n:
                    mine = lane // sz.cap == b
                    turn = (b - n) * sz.cap % LANES
                    tile_o = jnp.where(mine, pltpu.roll(offsets[b], turn, axis=1), tile_o)
                    tile_w = jnp.where(mine, pltpu.roll(weights[b], turn, axis=1), tile_w)
            o = jnp.bitwise_xor(m * packs + n, me)
            slot_offset[o] = tile_o.astype(jnp.int32)
            slot_weight[o] = tile_w
    for b in range(packs):
        slots = wide(b, sz.slot).astype(jnp.int32)
        taker_ref[b] = jnp.bitwise_xor(slots // sz.cap, me)
        place_ref[b] = slots % sz.cap + b * sz.cap
        for n in range(4):
            visc_ref[n, b] = wide(b, sz.visc + n * groups)
    basis = jnp.concatenate([line(b, sz.basis) for b in range(packs)], axis=0)
    terms = jnp.concatenate([line(b, sz.terms) for b in range(packs)], axis=0)
    kernel = lax.dot_general(
        basis, terms, (((1,), (1,)), ((), ())), precision=EXACT, preferred_element_type=jnp.float32
    )
    kernel_ref[...] = kernel

    sublane = lax.broadcasted_iota(jnp.int32, (SUB, LANES), 0)
    for ref, out in ((slot_offset, own_offset), (slot_weight, own_weight)):
        tile = jnp.zeros((SUB, LANES), out.dtype)
        for o in range(sz.blocks):
            here = (sublane == o // packs) & (lane // sz.cap == o % packs)
            turn = o % packs * sz.cap
            line_o = jnp.broadcast_to(ref[o, 0:1, :], (SUB, LANES))
            tile = jnp.where(here, pltpu.roll(line_o, turn, axis=1) if turn else line_o, tile)
        out[...] = tile

    upper = mixed(kernel, bottom_ref, fields)
    gather(sz, slot_offset, slot_weight, slot_value, top_ref, next_ref, taker_ref, place_ref, lower_ref)
    for c in range(fields):
        ghost_ref[0, c] = lower_ref[0, c]
        ghost_ref[1, c] = upper[c][0:SUB]
        for b in range(packs):
            outer_ref[0, b, c] = visc_ref[0, b] * upper[c][b * SUB : (b + 1) * SUB]
            outer_ref[1, b, c] = visc_ref[2, b] * lower_ref[b, c]


def couple_kernel(sz, me_ref, adv_hbm, coup_hbm, visc_hbm, even_ref, odd_ref, inside_hbm, out_hbm, *scratch):
    adv_ref, coup_ref, ends_ref, edge_ref, sems = scratch[:5]
    carried, work = scratch[5:-5], scratch[-5:]
    slot_offset, slot_weight, own_offset, own_weight, taker_ref, place_ref, kernel_ref, visc_ref, outer_ref, ghost_ref = carried
    slot_value, top_ref, next_ref, lower_ref, bottom_ref = work
    ends = [pl.ds(0, SUB), pl.ds(sz.rows - SUB, SUB)]
    pairs = [(adv_hbm, adv_ref), (coup_hbm, coup_ref)]
    pairs += [(visc_hbm.at[here, :], ends_ref.at[n]) for n, here in enumerate(ends)]
    pairs += [(inside_hbm.at[:, here, :], edge_ref.at[n]) for n, here in enumerate(ends)]
    arrived = fetch(pairs, sems)
    couple_first(sz, me_ref[0], even_ref, odd_ref, *carried, *work)
    packs, fields = sz.packs, sz.fields
    _, wide = faces_of(sz, even_ref, odd_ref, sz.first)
    kernel = kernel_ref[...]
    outer = {(n, b): [outer_ref[n, b, c] for c in range(fields)] for n in range(2) for b in range(packs)}
    inner = {}

    half = SUB // 2
    row = lax.broadcasted_iota(jnp.int32, (SUB, sz.width), 0)

    def ghosts_only(lower, upper):
        return [jnp.where(row == 0, lower[c], jnp.where(row == SUB - 1, upper[c], 0.0)) for c in range(fields)]

    for k in range(1, ITERS):
        for b in range(packs):
            for c in range(fields):
                top = wide(b, sz.top(k, c)) + outer[0, b][c]
                bottom = wide(b, sz.bottom(k, c)) + outer[1, b][c]
                keep_faces(sz, b, c, top, bottom, top_ref, next_ref, bottom_ref)
        if k == ITERS - 1:
            upper = mixed(kernel[:SUB], bottom_ref, fields)
            taker, place = taker_ref[0, 0:1, :], place_ref[0, 0:1, :]
            lower = gather_own(sz, own_offset[...], own_weight[...], top_ref, next_ref, taker, place)
        else:
            upper = mixed(kernel, bottom_ref, fields)
            gather(sz, slot_offset, slot_weight, slot_value, top_ref, next_ref, taker_ref, place_ref, lower_ref)
            lower = [lower_ref[0, c, 0:1, :] for c in range(fields)]
            if k == 1:
                arrived()
                own, speed = matrix_of(sz, adv_ref, coup_ref)
            for n in range(2):
                for b in range(packs):
                    e, e_in = outer[n, b], inner.get((n, b))
                    inner[n, b] = [visc_ref[2 * n + 1, b] * e[c] for c in range(fields)]

                    def column(c):
                        next_to = upper[c][b * SUB : (b + 1) * SUB] if n == 0 else lower_ref[b, c]
                        return next_to if e_in is None else next_to + e_in[c]

                    outer[n, b] = advance(sz, own, speed, e, visc_ref[2 * n, b], column, None)
        if k == 1:
            visc = PSEUDO * jnp.where(row < half, ends_ref[0], ends_ref[1])
            firsts = [[ghost_ref[n, c, 0:1, :] for c in range(fields)] for n in range(2)]
            forced = [visc * g for g in ghosts_only(*firsts)]
        ghost = ghosts_only(lower, [upper[c][0:1] for c in range(fields)])

        def around(c):
            return inside_column(forced[c]) + ghost[c]

        forced = advance(sz, own, speed, forced, visc, around, None)
    for c in range(fields):
        edge_ref[0, c] = edge_ref[0, c] + jnp.where(row < half, forced[c], 0.0)
        edge_ref[1, c] = edge_ref[1, c] + jnp.where(row >= half, forced[c], 0.0)
    fetch([(edge_ref.at[n], out_hbm.at[:, here, :]) for n, here in enumerate(ends)], sems)()


def spread(table, blocks, between):
    def swap(piece, mask):
        return lax.ppermute(piece, "blk", [(i, i ^ mask) for i in range(blocks)])

    parts, bit = [table], 4
    while bit < blocks:
        masks = [bit, 2 * bit, 3 * bit] if 2 * bit < blocks else [bit]
        have = jnp.concatenate(parts, axis=0) if len(parts) > 1 else parts[0]
        parts = [have] + [swap(have, mask) for mask in masks]
        bit = bit * (len(masks) + 1)
    parts[1] = between(parts[1])
    twos = [swap(part, 2) for part in parts]
    even = jnp.concatenate([t for pair in zip(parts, twos) for t in pair], axis=0)
    return even, swap(even, 1)


def per_device(
    state_now,
    time_source,
    viscosity,
    advection,
    coupling,
    owner_list,
    owner_offset,
    intersection_weight,
    phase_index,
):
    blocks = lax.axis_size("blk")
    fields, rows, width = state_now.shape
    arrays = (state_now, time_source, viscosity, advection, coupling)
    arrays += tuple(a.reshape(1, width) for a in (owner_list, owner_offset, intersection_weight))
    arrays = [pltpu.with_memory_space_constraint(a, pltpu.HBM) for a in arrays]
    state_now, time_source, viscosity, advection, coupling, owner_list, owner_offset, weight = arrays
    sz = Sizes(fields, rows, width, blocks)
    me = lax.axis_index("blk").astype(jnp.int32).reshape(1)
    smem = pl.BlockSpec(memory_space=pltpu.SMEM)
    vmem = pl.BlockSpec(memory_space=pltpu.VMEM)
    hbm = pl.BlockSpec(memory_space=pltpu.HBM)
    anywhere = pl.BlockSpec(memory_space=pl.ANY)
    f32, i32 = jnp.float32, jnp.int32
    scalars = [pltpu.SMEM((fields,), f32), pltpu.SMEM((fields, fields), f32)]
    block = jax.ShapeDtypeStruct((fields, rows, width), f32)
    limit = pltpu.CompilerParams(vmem_limit_bytes=50 * 1024 * 1024)
    two_ends = pltpu.VMEM((2, fields, SUB, width), f32)
    visc_ends = pltpu.VMEM((2, SUB, width), f32)
    table = pl.pallas_call(
        functools.partial(table_kernel, sz),
        out_shape=jax.ShapeDtypeStruct((sz.table, LANES), f32),
        in_specs=[smem] + [hbm] * 8,
        out_specs=vmem,
        scratch_shapes=scalars
        + [two_ends, two_ends, visc_ends]
        + [pltpu.VMEM((1, width), kind) for kind in (i32, i32, f32)]
        + [pltpu.SemaphoreType.DMA((11,))],
        compiler_params=limit,
    )(phase_index, advection, coupling, state_now, time_source, viscosity, owner_list, owner_offset, weight)
    insides = []

    def interior(piece):
        inside, piece = pl.pallas_call(
            functools.partial(interior_kernel, sz),
            out_shape=[block, jax.ShapeDtypeStruct(piece.shape, piece.dtype)],
            in_specs=[hbm] * 5 + [anywhere],
            out_specs=[hbm, anywhere],
            input_output_aliases={5: 1},
            scratch_shapes=scalars
            + [
                pltpu.VMEM((fields, rows, width), f32),
                pltpu.VMEM((fields, rows, width), f32),
                pltpu.VMEM((rows, width), f32),
                pltpu.VMEM((2, fields, rows, width), f32),
                pltpu.SemaphoreType.DMA((5,)),
            ],
            compiler_params=limit,
        )(advection, coupling, state_now, time_source, viscosity, piece)
        insides.append(inside)
        return piece

    even, odd = spread(table, blocks, interior)
    work = [
        pltpu.VMEM((blocks, fields, SUB, LANES), f32),
        pltpu.VMEM((sz.packs, sz.groups, fields, SUB, LANES), f32),
        pltpu.VMEM((sz.packs, sz.groups, fields, SUB, LANES), f32),
        pltpu.VMEM((sz.packs, fields, SUB, width), f32),
        pltpu.VMEM((fields, blocks, width), f32),
    ]
    carried = [
        pltpu.VMEM((blocks, SUB, LANES), i32),
        pltpu.VMEM((blocks, SUB, LANES), f32),
        pltpu.VMEM((SUB, LANES), i32),
        pltpu.VMEM((SUB, LANES), f32),
        pltpu.VMEM((sz.packs, SUB, width), i32),
        pltpu.VMEM((sz.packs, SUB, width), i32),
        pltpu.VMEM((blocks, blocks), f32),
        pltpu.VMEM((4, sz.packs, SUB, width), f32),
        pltpu.VMEM((2, sz.packs, fields, SUB, width), f32),
        pltpu.VMEM((2, fields, SUB, width), f32),
    ]
    return pl.pallas_call(
        functools.partial(couple_kernel, sz),
        out_shape=block,
        in_specs=[smem] + [hbm] * 3 + [vmem] * 2 + [hbm],
        out_specs=hbm,
        input_output_aliases={6: 0},
        scratch_shapes=scalars + [visc_ends, two_ends, pltpu.SemaphoreType.DMA((6,))] + carried + work,
        compiler_params=limit,
    )(me, advection, coupling, viscosity, even, odd, insides[0])


def solution(mesh):
    return jax.shard_map(
        per_device,
        mesh=mesh,
        in_specs=(
            P(None, None, ("groups", "blk")),
            P(None, None, ("groups", "blk")),
            P(None, ("groups", "blk")),
            P(),
            P(),
            P(("groups", "blk"), None),
            P(("groups", "blk")),
            P(("groups", "blk")),
            P(("groups", "blk")),
        ),
        out_specs=P(None, None, ("groups", "blk")),
        check_vma=False,
    )
```

```python
import functools
import math

import jax
import jax.numpy as jnp
from jax import lax
from jax.experimental import pallas as pl
from jax.experimental.pallas import tpu as pltpu
from jax.sharding import PartitionSpec as P

HARM = 8
PHASES = 512
LAG = 37
ITERS = 4
PSEUDO = 0.2
LANES = 128
SUB = 8
EXACT = lax.Precision.HIGHEST


class Sizes:
    def __init__(self, fields, rows, width, blocks):
        self.fields, self.rows, self.width, self.blocks = fields, rows, width, blocks
        self.groups = width // LANES
        self.cap = 2 * width // blocks
        self.packs = LANES // self.cap
        faces = fields * self.groups
        self.visc = 2 * faces
        self.slot = self.visc + 4 * self.groups
        self.offsets = self.slot + self.groups
        self.weights = self.offsets + SUB
        self.terms = self.weights + SUB
        self.basis = self.terms + 1
        self.first = -(-(self.basis + 1) // SUB) * SUB
        self.rest = -(-2 * (ITERS - 1) * faces // SUB) * SUB

        self.table = self.first + self.rest

    def top(self, k, c):
        return (2 * max(k - 1, 0) * self.fields + c) * self.groups

    def bottom(self, k, c):
        return self.top(k, c) + self.fields * self.groups


def matrix_of(sz, advection, coupling):
    own = [[-PSEUDO * coupling[c, d] for d in range(sz.fields)] for c in range(sz.fields)]
    speed = [PSEUDO * advection[c] for c in range(sz.fields)]
    for c in range(sz.fields):
        own[c][c] = own[c][c] + ((1.0 - 1.5 * PSEUDO) - speed[c])
    return own, speed


def shifted_west(u):
    lane = lax.broadcasted_iota(jnp.int32, u.shape, 1)
    return jnp.where(lane == 0, 0.0, pltpu.roll(u, 1, axis=1))


def shifted_east(u):
    width = u.shape[1]
    lane = lax.broadcasted_iota(jnp.int32, u.shape, 1)
    return jnp.where(lane == width - 1, 0.0, pltpu.roll(u, width - 1, axis=1))


def advance(sz, own, speed, u, visc, column, source):
    out = []
    for c in range(sz.fields):
        west, east = shifted_west(u[c]), shifted_east(u[c])
        new = speed[c] * west + visc * (west + east + column(c) - 4.0 * u[c])
        for d in range(sz.fields):
            new = new + own[c][d] * u[d]
        if source is not None:
            new = new - source(c)
        out.append(new)
    return out


def inside_column(u):
    row = lax.broadcasted_iota(jnp.int32, u.shape, 0)
    half = SUB // 2
    up = jnp.where((row == 0) | (row == half), 0.0, pltpu.roll(u, 1, axis=0))
    down = jnp.where((row == SUB - 1) | (row == half - 1), 0.0, pltpu.roll(u, SUB - 1, axis=0))
    return up + down


def in_parts(x):
    high = x.astype(jnp.bfloat16)
    rest = x - high.astype(jnp.float32)
    middle = rest.astype(jnp.bfloat16)
    low = (rest - middle.astype(jnp.float32)).astype(jnp.bfloat16)
    return high, middle, low


def fetch(pairs, sems):
    copies = [pltpu.make_async_copy(src, dst, sems.at[n]) for n, (src, dst) in enumerate(pairs)]
    for copy in copies:
        copy.start()

    def wait():
        for copy in copies:
            copy.wait()

    return wait


def edge_pairs(sz, state, source, viscosity, u_ref, q_ref, v_ref):
    pairs = []
    for n, first in enumerate((0, sz.rows - SUB)):
        here = pl.ds(first, SUB)
        pairs.append((state.at[:, here, :], u_ref.at[n]))
        pairs.append((source.at[:, here, :], q_ref.at[n]))
        pairs.append((viscosity.at[here, :], v_ref.at[n]))
    return pairs


def put(out_ref, at, row):
    for g in range(row.shape[1] // LANES):
        out_ref[at + g : at + g + 1, :] = row[:, g * LANES : (g + 1) * LANES]


def table_kernel(
    sz,
    phase_ref,
    adv_hbm,
    coup_hbm,
    state_hbm,
    source_hbm,
    visc_hbm,
    owner_hbm,
    offset_hbm,
    weight_hbm,
    out_ref,
    adv_ref,
    coup_ref,
    u_both,
    q_both,
    v_both,
    owner_ref,
    offset_ref,
    weight_ref,
    sems,
):
    pairs = [(owner_hbm, owner_ref), (offset_hbm, offset_ref), (weight_hbm, weight_ref)]
    lists_in = fetch(pairs, sems.at[pl.ds(0, 3)])
    pairs = edge_pairs(sz, state_hbm, source_hbm, visc_hbm, u_both, q_both, v_both)
    pairs += [(adv_hbm, adv_ref), (coup_hbm, coup_ref)]
    edges_in = fetch(pairs, sems.at[pl.ds(3, 8)])
    out_ref[sz.terms : sz.first, :] = jnp.zeros((sz.first - sz.terms, LANES), jnp.float32)
    order = lax.broadcasted_iota(jnp.int32, (1, LANES), 1)
    harmonic = jnp.where(order > HARM, order - HARM, order).astype(jnp.float32)
    used = order <= 2 * HARM

    def waves(angle):
        product = angle * harmonic
        return jnp.where(order <= HARM, jnp.cos(product), jnp.sin(product))

    phase = phase_ref[0].astype(jnp.float32)
    scale = jnp.where(order == 0, 1.0, 2.0) / sz.blocks
    terms = waves(phase * (2.0 * math.pi / PHASES)) * scale
    basis = waves((phase + LAG) * (2.0 * math.pi / PHASES))
    out_ref[sz.terms : sz.terms + 1, :] = jnp.where(used, terms, 0.0)
    out_ref[sz.basis : sz.basis + 1, :] = jnp.where(used, basis, 0.0)
    before = lax.broadcasted_iota(jnp.int32, (sz.width, sz.width), 0) <= lax.broadcasted_iota(
        jnp.int32, (sz.width, sz.width), 1
    )
    before = before.astype(jnp.bfloat16)
    lists_in()
    owner, offset, weight = owner_ref[...], offset_ref[...], weight_ref[...]
    member = lax.broadcasted_iota(jnp.int32, (sz.blocks, sz.width), 0) == owner
    member = member.astype(jnp.bfloat16)
    count = jnp.dot(member, before, preferred_element_type=jnp.float32)
    rank = jnp.sum(count * member.astype(jnp.float32), axis=0, keepdims=True) - 1.0
    rank = rank.astype(jnp.int32)
    slot = owner * sz.cap + rank
    put(out_ref, sz.slot, slot.astype(jnp.float32))
    place = (lax.broadcasted_iota(jnp.int32, (LANES, sz.width), 0) == slot % LANES).astype(jnp.bfloat16)
    held = lax.broadcasted_iota(jnp.int32, (SUB, sz.width), 0) == slot // LANES
    values = jnp.concatenate(
        [jnp.where(held, offset.astype(jnp.float32), 0.0), jnp.where(held, weight, 0.0)], axis=0
    )
    parts = jnp.concatenate(in_parts(values), axis=0)
    high, middle, low = jnp.split(
        lax.dot_general(parts, place, (((1,), (1,)), ((), ())), preferred_element_type=jnp.float32), 3, axis=0
    )
    out_ref[sz.offsets : sz.offsets + 2 * SUB, :] = high + (middle + low)

    edges_in()
    for c in range(sz.fields):
        put(out_ref, sz.top(0, c), u_both[1, c, SUB - 1 : SUB, :])
        put(out_ref, sz.bottom(0, c), u_both[0, c, 0:1, :])
    for n, (end, at) in enumerate(((1, SUB - 1), (1, SUB - 2), (0, 0), (0, 1))):
        put(out_ref, sz.visc + n * sz.groups, PSEUDO * v_both[end, at : at + 1, :])
    own, speed = matrix_of(sz, adv_ref, coup_ref)
    half = SUB // 2
    row = lax.broadcasted_iota(jnp.int32, (SUB, sz.width), 0)

    def both(low, high):
        return jnp.where(row < half, low, high)

    visc = PSEUDO * both(v_both[0], v_both[1])
    source = [PSEUDO * both(q_both[0, c], q_both[1, c]) for c in range(sz.fields)]
    u = [both(u_both[0, c], u_both[1, c]) for c in range(sz.fields)]
    for k in range(1, ITERS):
        u = advance(sz, own, speed, u, visc, lambda c: inside_column(u[c]), lambda c: source[c])
        for c in range(sz.fields):
            put(out_ref, sz.first + sz.top(k, c), u[c][SUB - 1 : SUB])
            put(out_ref, sz.first + sz.bottom(k, c), u[c][0:1])


def interior_kernel(
    sz,
    adv_hbm,
    coup_hbm,
    state_hbm,
    source_hbm,
    visc_hbm,
    after,
    out_hbm,
    passed,
    adv_ref,
    coup_ref,
    u_ref,
    q_ref,
    v_ref,
    work,
    sems,
):
    del after, passed
    pairs = [(adv_hbm, adv_ref), (coup_hbm, coup_ref), (state_hbm, u_ref), (source_hbm, q_ref), (visc_hbm, v_ref)]
    fetch(pairs, sems)()
    own, speed = matrix_of(sz, adv_ref, coup_ref)
    tiles = sz.rows // SUB
    row = lax.broadcasted_iota(jnp.int32, (SUB, sz.width), 0)
    for k in range(ITERS):
        src = u_ref if k == 0 else work.at[(k - 1) % 2]
        dst = work.at[k % 2]
        for t in range(tiles):
            here = slice(t * SUB, (t + 1) * SUB)
            u = [src[c, here, :] for c in range(sz.fields)]

            def column(c):
                up, down = pltpu.roll(u[c], 1, axis=0), pltpu.roll(u[c], SUB - 1, axis=0)
                above = src[c, t * SUB - 1 : t * SUB, :] if t > 0 else 0.0
                below = src[c, (t + 1) * SUB : (t + 1) * SUB + 1, :] if t < tiles - 1 else 0.0
                return jnp.where(row == 0, above, up) + jnp.where(row == SUB - 1, below, down)

            new = advance(sz, own, speed, u, PSEUDO * v_ref[here, :], column, lambda c: PSEUDO * q_ref[c, here, :])
            for c in range(sz.fields):
                dst[c, here, :] = new[c]
    fetch([(work.at[(ITERS - 1) % 2], out_hbm)], sems)()


def faces_of(sz, even_ref, odd_ref, base):
    def line(b, row):
        ref = (even_ref, odd_ref)[b % 2]
        return ref[pl.ds(b // 2 * sz.table + base + row, SUB, stride=sz.packs // 2 * sz.table), :]

    def wide(b, row):
        return jnp.concatenate([line(b, row + g) for g in range(sz.groups)], axis=1)

    return line, wide


def keep_faces(sz, b, c, top, bottom, top_ref, next_ref, bottom_ref):
    after = pltpu.roll(top, sz.width - 1, axis=1)
    for g in range(sz.groups):
        cells = slice(g * LANES, (g + 1) * LANES)
        top_ref[b, g, c] = top[:, cells]
        next_ref[b, g, c] = after[:, cells]
    bottom_ref[c, b * SUB : (b + 1) * SUB, :] = bottom


def gather(sz, slot_offset, slot_weight, slot_value, owner_value, top_ref, next_ref, taker_ref, place_ref, lower_ref):
    fields, groups = sz.fields, sz.groups
    def first_stage(sub, b, carry):
        o = sz.packs * sub + b
        offset, weight = slot_offset[o], slot_weight[o]
        at, part = offset % LANES, offset // LANES
        for c in range(fields):
            pair = []
            for ref in (top_ref, next_ref):
                value = None
                for g in range(groups):
                    source = jnp.broadcast_to(ref[b, g, c, sub : sub + 1, :], (SUB, LANES))
                    taken = jnp.take_along_axis(source, at, axis=1)
                    value = taken if value is None else jnp.where(part == g, taken, value)
                pair.append(value)
            slot_value[o, c] = weight * pair[0] + (1.0 - weight) * pair[1]
        return carry

    for sub in range(SUB):
        lax.fori_loop(0, sz.packs, functools.partial(first_stage, sub), 0, unroll=min(sz.packs, 2))
    lane = lax.broadcasted_iota(jnp.int32, (SUB, LANES), 1)
    for m in range(SUB):

        def regroup(b, carry):
            for c in range(fields):
                tile = None
                for n in range(sz.packs):
                    value = slot_value[m * sz.packs + n, c]
                    if not isinstance(b, int) or b != n:
                        value = pltpu.roll(value, (n - b) * sz.cap % LANES, axis=1)
                    tile = value if tile is None else jnp.where(lane // sz.cap == n, value, tile)
                owner_value[b, m, c] = tile
            return carry

        if sz.packs <= 4:
            for b in range(sz.packs):
                regroup(b, 0)
        else:
            lax.fori_loop(0, sz.packs, regroup, 0)
    for b in range(sz.packs):
        for g in range(groups):
            cells = slice(g * LANES, (g + 1) * LANES)
            taker, place = taker_ref[b, :, cells], place_ref[b, :, cells]
            found = [jnp.zeros((SUB, LANES), jnp.float32)] * fields
            for m in range(SUB):
                mine = taker == m
                for c in range(fields):
                    taken = jnp.take_along_axis(owner_value[b, m, c], place, axis=1)
                    found[c] = jnp.where(mine, taken, found[c])
            for c in range(fields):
                lower_ref[b, c, :, cells] = found[c]


def gather_own(sz, own_offset, own_weight, top_ref, next_ref, taker, place):
    fields, groups, packs = sz.fields, sz.groups, sz.packs
    lane = lax.broadcasted_iota(jnp.int32, (SUB, LANES), 1)
    at, part = own_offset % LANES, own_offset // LANES

    def stacked(row):
        parts = [row[:, g * LANES : (g + 1) * LANES] for g in range(groups)]
        return jnp.concatenate(parts + [parts[0]] * (SUB - groups), axis=0)

    taker, place = stacked(taker), stacked(place)
    ghost = []
    for c in range(fields):
        pair = []
        for ref in (top_ref, next_ref):
            value = jnp.zeros((SUB, LANES), jnp.float32)
            for b in range(packs):
                for g in range(groups):
                    source = ref[b, g, c]
                    here = (part == g) & (lane // sz.cap == b)
                    value = jnp.where(here, jnp.take_along_axis(source, at, axis=1), value)
            pair.append(value)
        held = own_weight * pair[0] + (1.0 - own_weight) * pair[1]
        found = jnp.zeros((SUB, LANES), jnp.float32)
        for m in range(SUB):
            source = jnp.broadcast_to(held[m : m + 1], (SUB, LANES))
            found = jnp.where(taker == m, jnp.take_along_axis(source, place, axis=1), found)
        ghost.append(jnp.concatenate([found[g : g + 1] for g in range(groups)], axis=1))
    return ghost


def mixed(kernel, bottom_ref, fields):
    high, middle, low = in_parts(kernel)
    left = jnp.concatenate([high, high, high, middle, middle, low], axis=1)
    out = []
    for c in range(fields):
        high, middle, low = in_parts(bottom_ref[c])
        right = jnp.concatenate([high, middle, low, high, middle, high], axis=0)
        out.append(jnp.dot(left, right, preferred_element_type=jnp.float32))
    return out


def couple_first(
    sz,
    me,
    even_ref,
    odd_ref,
    slot_offset,
    slot_weight,
    own_offset,
    own_weight,
    taker_ref,
    place_ref,
    kernel_ref,
    visc_ref,
    outer_ref,
    ghost_ref,
    slot_value,
    owner_value,
    top_ref,
    next_ref,
    lower_ref,
    bottom_ref,
):
    packs, groups, fields = sz.packs, sz.groups, sz.fields
    lane = lax.broadcasted_iota(jnp.int32, (SUB, LANES), 1)
    line, wide = faces_of(sz, even_ref, odd_ref, 0)
    for b in range(packs):
        for c in range(fields):
            top, bottom = wide(b, sz.top(0, c)), wide(b, sz.bottom(0, c))
            keep_faces(sz, b, c, top, bottom, top_ref, next_ref, bottom_ref)

    for m in range(SUB):
        offsets = [line(b, sz.offsets + m) for b in range(packs)]
        weights = [line(b, sz.weights + m) for b in range(packs)]
        for n in range(packs):
            tile_o, tile_w = offsets[n], weights[n]
            for b in range(packs):
                if b != n:
                    mine = lane // sz.cap == b
                    turn = (b - n) * sz.cap % LANES
                    tile_o = jnp.where(mine, pltpu.roll(offsets[b], turn, axis=1), tile_o)
                    tile_w = jnp.where(mine, pltpu.roll(weights[b], turn, axis=1), tile_w)
            o = jnp.bitwise_xor(m * packs + n, me)
            slot_offset[o] = tile_o.astype(jnp.int32)
            slot_weight[o] = tile_w
    for b in range(packs):
        slots = wide(b, sz.slot).astype(jnp.int32)
        owner = jnp.bitwise_xor(slots // sz.cap, me)
        taker_ref[b] = owner // packs
        place_ref[b] = owner % packs * sz.cap + slots % sz.cap
        for n in range(4):
            visc_ref[n, b] = wide(b, sz.visc + n * groups)
    basis = jnp.concatenate([line(b, sz.basis) for b in range(packs)], axis=0)
    terms = jnp.concatenate([line(b, sz.terms) for b in range(packs)], axis=0)
    kernel = lax.dot_general(
        basis, terms, (((1,), (1,)), ((), ())), precision=EXACT, preferred_element_type=jnp.float32
    )
    kernel_ref[...] = kernel

    sublane = lax.broadcasted_iota(jnp.int32, (SUB, LANES), 0)
    for ref, out in ((slot_offset, own_offset), (slot_weight, own_weight)):
        tile = jnp.zeros((SUB, LANES), out.dtype)
        for o in range(sz.blocks):
            here = (sublane == o // packs) & (lane // sz.cap == o % packs)
            turn = o % packs * sz.cap
            line_o = jnp.broadcast_to(ref[o, 0:1, :], (SUB, LANES))
            tile = jnp.where(here, pltpu.roll(line_o, turn, axis=1) if turn else line_o, tile)
        out[...] = tile

    upper = mixed(kernel, bottom_ref, fields)
    gather(sz, slot_offset, slot_weight, slot_value, owner_value, top_ref, next_ref, taker_ref, place_ref, lower_ref)
    for c in range(fields):
        ghost_ref[0, c] = lower_ref[0, c]
        ghost_ref[1, c] = upper[c][0:SUB]
        for b in range(packs):
            outer_ref[0, b, c] = visc_ref[0, b] * upper[c][b * SUB : (b + 1) * SUB]
            outer_ref[1, b, c] = visc_ref[2, b] * lower_ref[b, c]


def couple_kernel(sz, me_ref, adv_hbm, coup_hbm, visc_hbm, even_ref, odd_ref, inside_hbm, out_hbm, *scratch):
    adv_ref, coup_ref, ends_ref, edge_ref, sems = scratch[:5]
    carried, work = scratch[5:-6], scratch[-6:]
    slot_offset, slot_weight, own_offset, own_weight, taker_ref, place_ref, kernel_ref, visc_ref, outer_ref, ghost_ref = carried
    slot_value, owner_value, top_ref, next_ref, lower_ref, bottom_ref = work
    ends = [pl.ds(0, SUB), pl.ds(sz.rows - SUB, SUB)]
    pairs = [(adv_hbm, adv_ref), (coup_hbm, coup_ref)]
    pairs += [(visc_hbm.at[here, :], ends_ref.at[n]) for n, here in enumerate(ends)]
    pairs += [(inside_hbm.at[:, here, :], edge_ref.at[n]) for n, here in enumerate(ends)]
    arrived = fetch(pairs, sems)
    couple_first(sz, me_ref[0], even_ref, odd_ref, *carried, *work)
    packs, fields = sz.packs, sz.fields
    _, wide = faces_of(sz, even_ref, odd_ref, sz.first)
    kernel = kernel_ref[...]
    outer = {(n, b): [outer_ref[n, b, c] for c in range(fields)] for n in range(2) for b in range(packs)}
    inner = {}

    half = SUB // 2
    row = lax.broadcasted_iota(jnp.int32, (SUB, sz.width), 0)

    def ghosts_only(lower, upper):
        return [jnp.where(row == 0, lower[c], jnp.where(row == SUB - 1, upper[c], 0.0)) for c in range(fields)]

    for k in range(1, ITERS):
        for b in range(packs):
            for c in range(fields):
                top = wide(b, sz.top(k, c)) + outer[0, b][c]
                bottom = wide(b, sz.bottom(k, c)) + outer[1, b][c]
                keep_faces(sz, b, c, top, bottom, top_ref, next_ref, bottom_ref)
        if k == ITERS - 1:
            upper = mixed(kernel[:SUB], bottom_ref, fields)
            taker, place = taker_ref[0, 0:1, :], place_ref[0, 0:1, :]
            lower = gather_own(sz, own_offset[...], own_weight[...], top_ref, next_ref, taker, place)
        else:
            upper = mixed(kernel, bottom_ref, fields)
            gather(sz, slot_offset, slot_weight, slot_value, owner_value, top_ref, next_ref, taker_ref, place_ref, lower_ref)
            lower = [lower_ref[0, c, 0:1, :] for c in range(fields)]
            if k == 1:
                arrived()
                own, speed = matrix_of(sz, adv_ref, coup_ref)
            for n in range(2):
                for b in range(packs):
                    e, e_in = outer[n, b], inner.get((n, b))
                    inner[n, b] = [visc_ref[2 * n + 1, b] * e[c] for c in range(fields)]

                    def column(c):
                        next_to = upper[c][b * SUB : (b + 1) * SUB] if n == 0 else lower_ref[b, c]
                        return next_to if e_in is None else next_to + e_in[c]

                    outer[n, b] = advance(sz, own, speed, e, visc_ref[2 * n, b], column, None)
        if k == 1:
            visc = PSEUDO * jnp.where(row < half, ends_ref[0], ends_ref[1])
            firsts = [[ghost_ref[n, c, 0:1, :] for c in range(fields)] for n in range(2)]
            forced = [visc * g for g in ghosts_only(*firsts)]
        ghost = ghosts_only(lower, [upper[c][0:1] for c in range(fields)])

        def around(c):
            return inside_column(forced[c]) + ghost[c]

        forced = advance(sz, own, speed, forced, visc, around, None)
    for c in range(fields):
        edge_ref[0, c] = edge_ref[0, c] + jnp.where(row < half, forced[c], 0.0)
        edge_ref[1, c] = edge_ref[1, c] + jnp.where(row >= half, forced[c], 0.0)
    fetch([(edge_ref.at[n], out_hbm.at[:, here, :]) for n, here in enumerate(ends)], sems)()


def spread(table, blocks, between):
    def swap(piece, mask):
        return lax.ppermute(piece, "blk", [(i, i ^ mask) for i in range(blocks)])

    parts, bit = [table], 4
    while bit < blocks:
        masks = [bit, 2 * bit, 3 * bit] if 2 * bit < blocks else [bit]
        have = jnp.concatenate(parts, axis=0) if len(parts) > 1 else parts[0]
        parts = [have] + [swap(have, mask) for mask in masks]
        bit = bit * (len(masks) + 1)
    parts[1] = between(parts[1])
    twos = [swap(part, 2) for part in parts]
    even = jnp.concatenate([t for pair in zip(parts, twos) for t in pair], axis=0)
    return even, swap(even, 1)


def per_device(
    state_now,
    time_source,
    viscosity,
    advection,
    coupling,
    owner_list,
    owner_offset,
    intersection_weight,
    phase_index,
):
    blocks = lax.axis_size("blk")
    fields, rows, width = state_now.shape
    arrays = (state_now, time_source, viscosity, advection, coupling)
    arrays += tuple(a.reshape(1, width) for a in (owner_list, owner_offset, intersection_weight))
    arrays = [pltpu.with_memory_space_constraint(a, pltpu.HBM) for a in arrays]
    state_now, time_source, viscosity, advection, coupling, owner_list, owner_offset, weight = arrays
    sz = Sizes(fields, rows, width, blocks)
    me = lax.axis_index("blk").astype(jnp.int32).reshape(1)
    smem = pl.BlockSpec(memory_space=pltpu.SMEM)
    vmem = pl.BlockSpec(memory_space=pltpu.VMEM)
    hbm = pl.BlockSpec(memory_space=pltpu.HBM)
    anywhere = pl.BlockSpec(memory_space=pl.ANY)
    f32, i32 = jnp.float32, jnp.int32
    scalars = [pltpu.SMEM((fields,), f32), pltpu.SMEM((fields, fields), f32)]
    block = jax.ShapeDtypeStruct((fields, rows, width), f32)
    limit = pltpu.CompilerParams(vmem_limit_bytes=50 * 1024 * 1024)
    two_ends = pltpu.VMEM((2, fields, SUB, width), f32)
    visc_ends = pltpu.VMEM((2, SUB, width), f32)
    table = pl.pallas_call(
        functools.partial(table_kernel, sz),
        out_shape=jax.ShapeDtypeStruct((sz.table, LANES), f32),
        in_specs=[smem] + [hbm] * 8,
        out_specs=vmem,
        scratch_shapes=scalars
        + [two_ends, two_ends, visc_ends]
        + [pltpu.VMEM((1, width), kind) for kind in (i32, i32, f32)]
        + [pltpu.SemaphoreType.DMA((11,))],
        compiler_params=limit,
    )(phase_index, advection, coupling, state_now, time_source, viscosity, owner_list, owner_offset, weight)
    insides = []

    def interior(piece):
        inside, piece = pl.pallas_call(
            functools.partial(interior_kernel, sz),
            out_shape=[block, jax.ShapeDtypeStruct(piece.shape, piece.dtype)],
            in_specs=[hbm] * 5 + [anywhere],
            out_specs=[hbm, anywhere],
            input_output_aliases={5: 1},
            scratch_shapes=scalars
            + [
                pltpu.VMEM((fields, rows, width), f32),
                pltpu.VMEM((fields, rows, width), f32),
                pltpu.VMEM((rows, width), f32),
                pltpu.VMEM((2, fields, rows, width), f32),
                pltpu.SemaphoreType.DMA((5,)),
            ],
            compiler_params=limit,
        )(advection, coupling, state_now, time_source, viscosity, piece)
        insides.append(inside)
        return piece

    even, odd = spread(table, blocks, interior)
    work = [
        pltpu.VMEM((blocks, fields, SUB, LANES), f32),
        pltpu.VMEM((sz.packs, SUB, fields, SUB, LANES), f32),
        pltpu.VMEM((sz.packs, sz.groups, fields, SUB, LANES), f32),
        pltpu.VMEM((sz.packs, sz.groups, fields, SUB, LANES), f32),
        pltpu.VMEM((sz.packs, fields, SUB, width), f32),
        pltpu.VMEM((fields, blocks, width), f32),
    ]
    carried = [
        pltpu.VMEM((blocks, SUB, LANES), i32),
        pltpu.VMEM((blocks, SUB, LANES), f32),
        pltpu.VMEM((SUB, LANES), i32),
        pltpu.VMEM((SUB, LANES), f32),
        pltpu.VMEM((sz.packs, SUB, width), i32),
        pltpu.VMEM((sz.packs, SUB, width), i32),
        pltpu.VMEM((blocks, blocks), f32),
        pltpu.VMEM((4, sz.packs, SUB, width), f32),
        pltpu.VMEM((2, sz.packs, fields, SUB, width), f32),
        pltpu.VMEM((2, fields, SUB, width), f32),
    ]
    return pl.pallas_call(
        functools.partial(couple_kernel, sz),
        out_shape=block,
        in_specs=[smem] + [hbm] * 3 + [vmem] * 2 + [hbm],
        out_specs=hbm,
        input_output_aliases={6: 0},
        scratch_shapes=scalars + [visc_ends, two_ends, pltpu.SemaphoreType.DMA((6,))] + carried + work,
        compiler_params=limit,
    )(me, advection, coupling, viscosity, even, odd, insides[0])


def solution(mesh):
    return jax.shard_map(
        per_device,
        mesh=mesh,
        in_specs=(
            P(None, None, ("groups", "blk")),
            P(None, None, ("groups", "blk")),
            P(None, ("groups", "blk")),
            P(),
            P(),
            P(("groups", "blk"), None),
            P(("groups", "blk")),
            P(("groups", "blk")),
            P(("groups", "blk")),
        ),
        out_specs=P(None, None, ("groups", "blk")),
        check_vma=False,
    )
```

```python
import functools
import math

import jax
import jax.numpy as jnp
from jax import lax
from jax.experimental import pallas as pl
from jax.experimental.pallas import tpu as pltpu
from jax.sharding import PartitionSpec as P

HARM = 8
PHASES = 512
LAG = 37
ITERS = 4
PSEUDO = 0.2
LANES = 128
SUB = 8
EXACT = lax.Precision.HIGHEST


class Sizes:
    def __init__(self, fields, rows, width, blocks):
        self.fields, self.rows, self.width, self.blocks = fields, rows, width, blocks
        self.groups = width // LANES
        self.cap = 2 * width // blocks
        self.packs = LANES // self.cap
        faces = fields * self.groups
        self.visc = 2 * faces
        self.slot = self.visc + 4 * self.groups
        self.offsets = self.slot + self.groups
        self.weights = self.offsets + SUB
        self.terms = self.weights + SUB
        self.basis = self.terms + 1
        self.first = -(-(self.basis + 2) // SUB) * SUB
        self.rest = -(-2 * (ITERS - 1) * faces // SUB) * SUB

        self.table = self.first + self.rest

    def top(self, k, c):
        return (2 * max(k - 1, 0) * self.fields + c) * self.groups

    def bottom(self, k, c):
        return self.top(k, c) + self.fields * self.groups


def matrix_of(sz, advection, coupling):
    own = [[-PSEUDO * coupling[c, d] for d in range(sz.fields)] for c in range(sz.fields)]
    speed = [PSEUDO * advection[c] for c in range(sz.fields)]
    for c in range(sz.fields):
        own[c][c] = own[c][c] + ((1.0 - 1.5 * PSEUDO) - speed[c])
    return own, speed


def shifted_west(u):
    lane = lax.broadcasted_iota(jnp.int32, u.shape, 1)
    return jnp.where(lane == 0, 0.0, pltpu.roll(u, 1, axis=1))


def shifted_east(u):
    width = u.shape[1]
    lane = lax.broadcasted_iota(jnp.int32, u.shape, 1)
    return jnp.where(lane == width - 1, 0.0, pltpu.roll(u, width - 1, axis=1))


def advance(sz, own, speed, u, visc, column, source):
    out = []
    for c in range(sz.fields):
        west, east = shifted_west(u[c]), shifted_east(u[c])
        new = speed[c] * west + visc * (west + east + column(c) - 4.0 * u[c])
        for d in range(sz.fields):
            new = new + own[c][d] * u[d]
        if source is not None:
            new = new - source(c)
        out.append(new)
    return out


def inside_column(u):
    row = lax.broadcasted_iota(jnp.int32, u.shape, 0)
    half = SUB // 2
    up = jnp.where((row == 0) | (row == half), 0.0, pltpu.roll(u, 1, axis=0))
    down = jnp.where((row == SUB - 1) | (row == half - 1), 0.0, pltpu.roll(u, SUB - 1, axis=0))
    return up + down


def in_parts(x):
    high = x.astype(jnp.bfloat16)
    rest = x - high.astype(jnp.float32)
    middle = rest.astype(jnp.bfloat16)
    low = (rest - middle.astype(jnp.float32)).astype(jnp.bfloat16)
    return high, middle, low


def fetch(pairs, sems):
    copies = [pltpu.make_async_copy(src, dst, sems.at[n]) for n, (src, dst) in enumerate(pairs)]
    for copy in copies:
        copy.start()

    def wait():
        for copy in copies:
            copy.wait()

    return wait


def edge_pairs(sz, state, source, viscosity, u_ref, q_ref, v_ref):
    pairs = []
    for n, first in enumerate((0, sz.rows - SUB)):
        here = pl.ds(first, SUB)
        pairs.append((state.at[:, here, :], u_ref.at[n]))
        pairs.append((source.at[:, here, :], q_ref.at[n]))
        pairs.append((viscosity.at[here, :], v_ref.at[n]))
    return pairs


def put(out_ref, at, row):
    for g in range(row.shape[1] // LANES):
        out_ref[at + g : at + g + 1, :] = row[:, g * LANES : (g + 1) * LANES]


def table_kernel(
    sz,
    phase_ref,
    adv_hbm,
    coup_hbm,
    state_hbm,
    source_hbm,
    visc_hbm,
    owner_hbm,
    offset_hbm,
    weight_hbm,
    out_ref,
    adv_ref,
    coup_ref,
    u_both,
    q_both,
    v_both,
    owner_ref,
    offset_ref,
    weight_ref,
    sems,
):
    pairs = [(owner_hbm, owner_ref), (offset_hbm, offset_ref), (weight_hbm, weight_ref)]
    lists_in = fetch(pairs, sems.at[pl.ds(0, 3)])
    pairs = edge_pairs(sz, state_hbm, source_hbm, visc_hbm, u_both, q_both, v_both)
    pairs += [(adv_hbm, adv_ref), (coup_hbm, coup_ref)]
    edges_in = fetch(pairs, sems.at[pl.ds(3, 8)])
    out_ref[sz.terms : sz.first, :] = jnp.zeros((sz.first - sz.terms, LANES), jnp.float32)
    order = lax.broadcasted_iota(jnp.int32, (1, LANES), 1)
    harmonic = jnp.where(order > HARM, order - HARM, order).astype(jnp.float32)
    used = order <= 2 * HARM

    def waves(angle):
        product = angle * harmonic
        return jnp.where(order <= HARM, jnp.cos(product), jnp.sin(product))

    phase = phase_ref[0].astype(jnp.float32)
    scale = jnp.where(order == 0, 1.0, 2.0) / sz.blocks
    terms = waves(phase * (2.0 * math.pi / PHASES)) * scale
    basis = waves((phase + LAG) * (2.0 * math.pi / PHASES))
    out_ref[sz.terms : sz.terms + 1, :] = jnp.where(used, terms, 0.0)
    out_ref[sz.basis : sz.basis + 1, :] = jnp.where(used, basis, 0.0)
    before = lax.broadcasted_iota(jnp.int32, (sz.width, sz.width), 0) <= lax.broadcasted_iota(
        jnp.int32, (sz.width, sz.width), 1
    )
    before = before.astype(jnp.bfloat16)
    lists_in()
    owner, offset, weight = owner_ref[...], offset_ref[...], weight_ref[...]
    member = lax.broadcasted_iota(jnp.int32, (sz.blocks, sz.width), 0) == owner
    member = member.astype(jnp.bfloat16)
    count = jnp.dot(member, before, preferred_element_type=jnp.float32)
    rank = jnp.sum(count * member.astype(jnp.float32), axis=0, keepdims=True) - 1.0
    rank = rank.astype(jnp.int32)
    slot = owner * sz.cap + rank
    put(out_ref, sz.slot, slot.astype(jnp.float32))
    place = (lax.broadcasted_iota(jnp.int32, (LANES, sz.width), 0) == slot % LANES).astype(jnp.bfloat16)
    held = lax.broadcasted_iota(jnp.int32, (SUB, sz.width), 0) == slot // LANES
    values = jnp.concatenate(
        [jnp.where(held, offset.astype(jnp.float32), 0.0), jnp.where(held, weight, 0.0)], axis=0
    )
    parts = jnp.concatenate(in_parts(values), axis=0)
    high, middle, low = jnp.split(
        lax.dot_general(parts, place, (((1,), (1,)), ((), ())), preferred_element_type=jnp.float32), 3, axis=0
    )
    out_ref[sz.offsets : sz.offsets + 2 * SUB, :] = high + (middle + low)

    edges_in()
    for c in range(sz.fields):
        put(out_ref, sz.top(0, c), u_both[1, c, SUB - 1 : SUB, :])
        put(out_ref, sz.bottom(0, c), u_both[0, c, 0:1, :])
    for n, (end, at) in enumerate(((1, SUB - 1), (1, SUB - 2), (0, 0), (0, 1))):
        put(out_ref, sz.visc + n * sz.groups, PSEUDO * v_both[end, at : at + 1, :])
    own, speed = matrix_of(sz, adv_ref, coup_ref)
    half = SUB // 2
    row = lax.broadcasted_iota(jnp.int32, (SUB, sz.width), 0)

    def both(low, high):
        return jnp.where(row < half, low, high)

    visc = PSEUDO * both(v_both[0], v_both[1])
    source = [PSEUDO * both(q_both[0, c], q_both[1, c]) for c in range(sz.fields)]
    u = [both(u_both[0, c], u_both[1, c]) for c in range(sz.fields)]
    for k in range(1, ITERS):
        u = advance(sz, own, speed, u, visc, lambda c: inside_column(u[c]), lambda c: source[c])
        for c in range(sz.fields):
            put(out_ref, sz.first + sz.top(k, c), u[c][SUB - 1 : SUB])
            put(out_ref, sz.first + sz.bottom(k, c), u[c][0:1])


def interior_kernel(
    sz,
    adv_hbm,
    coup_hbm,
    state_hbm,
    source_hbm,
    visc_hbm,
    after,
    out_hbm,
    passed,
    adv_ref,
    coup_ref,
    u_ref,
    q_ref,
    v_ref,
    work,
    sems,
):
    del after, passed
    pairs = [(adv_hbm, adv_ref), (coup_hbm, coup_ref), (state_hbm, u_ref), (source_hbm, q_ref), (visc_hbm, v_ref)]
    fetch(pairs, sems)()
    own, speed = matrix_of(sz, adv_ref, coup_ref)
    tiles = sz.rows // SUB
    row = lax.broadcasted_iota(jnp.int32, (SUB, sz.width), 0)
    for k in range(ITERS):
        src = u_ref if k == 0 else work.at[(k - 1) % 2]
        dst = work.at[k % 2]
        for t in range(tiles):
            here = slice(t * SUB, (t + 1) * SUB)
            u = [src[c, here, :] for c in range(sz.fields)]

            def column(c):
                up, down = pltpu.roll(u[c], 1, axis=0), pltpu.roll(u[c], SUB - 1, axis=0)
                above = src[c, t * SUB - 1 : t * SUB, :] if t > 0 else 0.0
                below = src[c, (t + 1) * SUB : (t + 1) * SUB + 1, :] if t < tiles - 1 else 0.0
                return jnp.where(row == 0, above, up) + jnp.where(row == SUB - 1, below, down)

            new = advance(sz, own, speed, u, PSEUDO * v_ref[here, :], column, lambda c: PSEUDO * q_ref[c, here, :])
            for c in range(sz.fields):
                dst[c, here, :] = new[c]
    fetch([(work.at[(ITERS - 1) % 2], out_hbm)], sems)()


def faces_of(sz, even_ref, odd_ref, base):
    def line(b, row):
        ref = (even_ref, odd_ref)[b % 2]
        return ref[pl.ds(b // 2 * sz.table + base + row, SUB, stride=sz.packs // 2 * sz.table), :]

    def wide(b, row):
        return jnp.concatenate([line(b, row + g) for g in range(sz.groups)], axis=1)

    return line, wide


def keep_faces(sz, b, c, top, bottom, top_ref, next_ref, bottom_ref):
    after = pltpu.roll(top, sz.width - 1, axis=1)
    for g in range(sz.groups):
        cells = slice(g * LANES, (g + 1) * LANES)
        top_ref[b, g, c] = top[:, cells]
        next_ref[b, g, c] = after[:, cells]
    bottom_ref[c, b * SUB : (b + 1) * SUB, :] = bottom


def gather(sz, slot_offset, slot_weight, slot_value, owner_value, top_ref, next_ref, taker_ref, place_ref, lower_ref):
    fields, groups = sz.fields, sz.groups
    def first_stage(sub, b, carry):
        o = sz.packs * sub + b
        offset, weight = slot_offset[o], slot_weight[o]
        at, part = offset % LANES, offset // LANES
        for c in range(fields):
            pair = []
            for ref in (top_ref, next_ref):
                value = None
                for g in range(groups):
                    source = jnp.broadcast_to(ref[b, g, c, sub : sub + 1, :], (SUB, LANES))
                    taken = jnp.take_along_axis(source, at, axis=1)
                    value = taken if value is None else jnp.where(part == g, taken, value)
                pair.append(value)
            slot_value[o, c] = weight * pair[0] + (1.0 - weight) * pair[1]
        return carry

    for sub in range(SUB):
        lax.fori_loop(0, sz.packs, functools.partial(first_stage, sub), 0, unroll=min(sz.packs, 2))
    lane = lax.broadcasted_iota(jnp.int32, (SUB, LANES), 1)
    for m in range(SUB):

        def regroup(b, carry):
            for c in range(fields):
                tile = None
                for n in range(sz.packs):
                    value = slot_value[m * sz.packs + n, c]
                    if not isinstance(b, int) or b != n:
                        value = pltpu.roll(value, (n - b) * sz.cap % LANES, axis=1)
                    tile = value if tile is None else jnp.where(lane // sz.cap == n, value, tile)
                owner_value[b, m, c] = tile
            return carry

        if sz.packs <= 4:
            for b in range(sz.packs):
                regroup(b, 0)
        else:
            lax.fori_loop(0, sz.packs, regroup, 0)
    for b in range(sz.packs):
        for g in range(groups):
            cells = slice(g * LANES, (g + 1) * LANES)
            taker, place = taker_ref[b, :, cells], place_ref[b, :, cells]
            found = [jnp.zeros((SUB, LANES), jnp.float32)] * fields
            for m in range(SUB):
                mine = taker == m
                for c in range(fields):
                    taken = jnp.take_along_axis(owner_value[b, m, c], place, axis=1)
                    found[c] = jnp.where(mine, taken, found[c])
            for c in range(fields):
                lower_ref[b, c, :, cells] = found[c]


def gather_own(sz, own_offset, own_weight, top_ref, next_ref, taker, place):
    fields, groups, packs = sz.fields, sz.groups, sz.packs
    lane = lax.broadcasted_iota(jnp.int32, (SUB, LANES), 1)
    at, part = own_offset % LANES, own_offset // LANES

    def stacked(row):
        parts = [row[:, g * LANES : (g + 1) * LANES] for g in range(groups)]
        return jnp.concatenate(parts + [parts[0]] * (SUB - groups), axis=0)

    taker, place = stacked(taker), stacked(place)
    ghost = []
    for c in range(fields):
        pair = []
        for ref in (top_ref, next_ref):
            value = jnp.zeros((SUB, LANES), jnp.float32)
            for b in range(packs):
                for g in range(groups):
                    source = ref[b, g, c]
                    here = (part == g) & (lane // sz.cap == b)
                    value = jnp.where(here, jnp.take_along_axis(source, at, axis=1), value)
            pair.append(value)
        held = own_weight * pair[0] + (1.0 - own_weight) * pair[1]
        found = jnp.zeros((SUB, LANES), jnp.float32)
        for m in range(SUB):
            source = jnp.broadcast_to(held[m : m + 1], (SUB, LANES))
            found = jnp.where(taker == m, jnp.take_along_axis(source, place, axis=1), found)
        ghost.append(jnp.concatenate([found[g : g + 1] for g in range(groups)], axis=1))
    return ghost


def mixed(kernel, bottom_ref, fields):
    high, middle, low = in_parts(kernel)
    left = jnp.concatenate([high, high, high, middle, middle, low], axis=1)
    out = []
    for c in range(fields):
        high, middle, low = in_parts(bottom_ref[c])
        right = jnp.concatenate([high, middle, low, high, middle, high], axis=0)
        out.append(jnp.dot(left, right, preferred_element_type=jnp.float32))
    return out


def couple_first(
    sz,
    me,
    even_ref,
    odd_ref,
    slot_offset,
    slot_weight,
    own_offset,
    own_weight,
    taker_ref,
    place_ref,
    kernel_ref,
    visc_ref,
    outer_ref,
    ghost_ref,
    slot_value,
    owner_value,
    top_ref,
    next_ref,
    lower_ref,
    bottom_ref,
):
    packs, groups, fields = sz.packs, sz.groups, sz.fields
    lane = lax.broadcasted_iota(jnp.int32, (SUB, LANES), 1)
    line, wide = faces_of(sz, even_ref, odd_ref, 0)
    for b in range(packs):
        for c in range(fields):
            top, bottom = wide(b, sz.top(0, c)), wide(b, sz.bottom(0, c))
            keep_faces(sz, b, c, top, bottom, top_ref, next_ref, bottom_ref)

    for m in range(SUB):
        offsets = [line(b, sz.offsets + m) for b in range(packs)]
        weights = [line(b, sz.weights + m) for b in range(packs)]
        for n in range(packs):
            tile_o, tile_w = offsets[n], weights[n]
            for b in range(packs):
                if b != n:
                    mine = lane // sz.cap == b
                    turn = (b - n) * sz.cap % LANES
                    tile_o = jnp.where(mine, pltpu.roll(offsets[b], turn, axis=1), tile_o)
                    tile_w = jnp.where(mine, pltpu.roll(weights[b], turn, axis=1), tile_w)
            o = jnp.bitwise_xor(m * packs + n, me)
            slot_offset[o] = tile_o.astype(jnp.int32)
            slot_weight[o] = tile_w
    for b in range(packs):
        slots = wide(b, sz.slot).astype(jnp.int32)
        owner = jnp.bitwise_xor(slots // sz.cap, me)
        taker_ref[b] = owner // packs
        place_ref[b] = owner % packs * sz.cap + slots % sz.cap
        for n in range(4):
            visc_ref[n, b] = wide(b, sz.visc + n * groups)
    basis = jnp.concatenate([line(b, sz.basis) for b in range(packs)], axis=0)
    terms = jnp.concatenate([line(b, sz.terms) for b in range(packs)], axis=0)
    kernel = lax.dot_general(
        basis, terms, (((1,), (1,)), ((), ())), precision=EXACT, preferred_element_type=jnp.float32
    )
    kernel_ref[...] = kernel

    sublane = lax.broadcasted_iota(jnp.int32, (SUB, LANES), 0)
    for ref, out in ((slot_offset, own_offset), (slot_weight, own_weight)):
        tile = jnp.zeros((SUB, LANES), out.dtype)
        for o in range(sz.blocks):
            here = (sublane == o // packs) & (lane // sz.cap == o % packs)
            turn = o % packs * sz.cap
            line_o = jnp.broadcast_to(ref[o, 0:1, :], (SUB, LANES))
            tile = jnp.where(here, pltpu.roll(line_o, turn, axis=1) if turn else line_o, tile)
        out[...] = tile

    upper = mixed(kernel, bottom_ref, fields)
    gather(sz, slot_offset, slot_weight, slot_value, owner_value, top_ref, next_ref, taker_ref, place_ref, lower_ref)
    for c in range(fields):
        ghost_ref[0, c] = lower_ref[0, c]
        ghost_ref[1, c] = upper[c][0:SUB]
        for b in range(packs):
            outer_ref[0, b, c] = visc_ref[0, b] * upper[c][b * SUB : (b + 1) * SUB]
            outer_ref[1, b, c] = visc_ref[2, b] * lower_ref[b, c]


def couple_kernel(sz, me_ref, adv_hbm, coup_hbm, visc_hbm, even_ref, odd_ref, inside_hbm, out_hbm, *scratch):
    adv_ref, coup_ref, ends_ref, edge_ref, sems = scratch[:5]
    carried, work = scratch[5:-6], scratch[-6:]
    slot_offset, slot_weight, own_offset, own_weight, taker_ref, place_ref, kernel_ref, visc_ref, outer_ref, ghost_ref = carried
    slot_value, owner_value, top_ref, next_ref, lower_ref, bottom_ref = work
    ends = [pl.ds(0, SUB), pl.ds(sz.rows - SUB, SUB)]
    pairs = [(adv_hbm, adv_ref), (coup_hbm, coup_ref)]
    pairs += [(visc_hbm.at[here, :], ends_ref.at[n]) for n, here in enumerate(ends)]
    pairs += [(inside_hbm.at[:, here, :], edge_ref.at[n]) for n, here in enumerate(ends)]
    arrived = fetch(pairs, sems)
    couple_first(sz, me_ref[0], even_ref, odd_ref, *carried, *work)
    packs, fields = sz.packs, sz.fields
    _, wide = faces_of(sz, even_ref, odd_ref, sz.first)
    kernel = kernel_ref[...]
    outer = {(n, b): [outer_ref[n, b, c] for c in range(fields)] for n in range(2) for b in range(packs)}
    inner = {}

    half = SUB // 2
    row = lax.broadcasted_iota(jnp.int32, (SUB, sz.width), 0)

    def ghosts_only(lower, upper):
        return [jnp.where(row == 0, lower[c], jnp.where(row == SUB - 1, upper[c], 0.0)) for c in range(fields)]

    for k in range(1, ITERS):
        for b in range(packs):
            for c in range(fields):
                top = wide(b, sz.top(k, c)) + outer[0, b][c]
                bottom = wide(b, sz.bottom(k, c)) + outer[1, b][c]
                keep_faces(sz, b, c, top, bottom, top_ref, next_ref, bottom_ref)
        if k == ITERS - 1:
            upper = mixed(kernel[:SUB], bottom_ref, fields)
            taker, place = taker_ref[0, 0:1, :], place_ref[0, 0:1, :]
            lower = gather_own(sz, own_offset[...], own_weight[...], top_ref, next_ref, taker, place)
        else:
            upper = mixed(kernel, bottom_ref, fields)
            gather(sz, slot_offset, slot_weight, slot_value, owner_value, top_ref, next_ref, taker_ref, place_ref, lower_ref)
            lower = [lower_ref[0, c, 0:1, :] for c in range(fields)]
            if k == 1:
                arrived()
                own, speed = matrix_of(sz, adv_ref, coup_ref)
            for n in range(2):
                for b in range(packs):
                    e, e_in = outer[n, b], inner.get((n, b))
                    inner[n, b] = [visc_ref[2 * n + 1, b] * e[c] for c in range(fields)]

                    def column(c):
                        next_to = upper[c][b * SUB : (b + 1) * SUB] if n == 0 else lower_ref[b, c]
                        return next_to if e_in is None else next_to + e_in[c]

                    outer[n, b] = advance(sz, own, speed, e, visc_ref[2 * n, b], column, None)
        if k == 1:
            visc = PSEUDO * jnp.where(row < half, ends_ref[0], ends_ref[1])
            firsts = [[ghost_ref[n, c, 0:1, :] for c in range(fields)] for n in range(2)]
            forced = [visc * g for g in ghosts_only(*firsts)]
        ghost = ghosts_only(lower, [upper[c][0:1] for c in range(fields)])

        def around(c):
            return inside_column(forced[c]) + ghost[c]

        forced = advance(sz, own, speed, forced, visc, around, None)
    for c in range(fields):
        edge_ref[0, c] = edge_ref[0, c] + jnp.where(row < half, forced[c], 0.0)
        edge_ref[1, c] = edge_ref[1, c] + jnp.where(row >= half, forced[c], 0.0)
    fetch([(edge_ref.at[n], out_hbm.at[:, here, :]) for n, here in enumerate(ends)], sems)()


def spread(table, blocks, spare, between):
    def swap(piece, mask):
        return lax.ppermute(piece, "blk", [(i, i ^ mask) for i in range(blocks)])

    parts, bit = [table], 4
    while bit < blocks:
        masks = [bit, 2 * bit, 3 * bit] if 2 * bit < blocks else [bit]
        have = jnp.concatenate(parts, axis=0) if len(parts) > 1 else parts[0]
        parts = [have] + [swap(have, mask) for mask in masks]
        bit = bit * (len(masks) + 1)
    twos = [between(swap(parts[0], 2))]
    parts[1:] = [part.at[spare].set(twos[0][spare]) for part in parts[1:]]
    twos += [swap(part, 2) for part in parts[1:]]
    even = jnp.concatenate([t for pair in zip(parts, twos) for t in pair], axis=0)
    return even, swap(even, 1)


def per_device(
    state_now,
    time_source,
    viscosity,
    advection,
    coupling,
    owner_list,
    owner_offset,
    intersection_weight,
    phase_index,
):
    blocks = lax.axis_size("blk")
    fields, rows, width = state_now.shape
    arrays = (state_now, time_source, viscosity, advection, coupling)
    arrays += tuple(a.reshape(1, width) for a in (owner_list, owner_offset, intersection_weight))
    arrays = [pltpu.with_memory_space_constraint(a, pltpu.HBM) for a in arrays]
    state_now, time_source, viscosity, advection, coupling, owner_list, owner_offset, weight = arrays
    sz = Sizes(fields, rows, width, blocks)
    me = lax.axis_index("blk").astype(jnp.int32).reshape(1)
    smem = pl.BlockSpec(memory_space=pltpu.SMEM)
    vmem = pl.BlockSpec(memory_space=pltpu.VMEM)
    hbm = pl.BlockSpec(memory_space=pltpu.HBM)
    anywhere = pl.BlockSpec(memory_space=pl.ANY)
    f32, i32 = jnp.float32, jnp.int32
    scalars = [pltpu.SMEM((fields,), f32), pltpu.SMEM((fields, fields), f32)]
    block = jax.ShapeDtypeStruct((fields, rows, width), f32)
    limit = pltpu.CompilerParams(vmem_limit_bytes=50 * 1024 * 1024)
    two_ends = pltpu.VMEM((2, fields, SUB, width), f32)
    visc_ends = pltpu.VMEM((2, SUB, width), f32)
    table = pl.pallas_call(
        functools.partial(table_kernel, sz),
        out_shape=jax.ShapeDtypeStruct((sz.table, LANES), f32),
        in_specs=[smem] + [hbm] * 8,
        out_specs=vmem,
        scratch_shapes=scalars
        + [two_ends, two_ends, visc_ends]
        + [pltpu.VMEM((1, width), kind) for kind in (i32, i32, f32)]
        + [pltpu.SemaphoreType.DMA((11,))],
        compiler_params=limit,
    )(phase_index, advection, coupling, state_now, time_source, viscosity, owner_list, owner_offset, weight)
    insides = []

    def interior(piece):
        inside, piece = pl.pallas_call(
            functools.partial(interior_kernel, sz),
            out_shape=[block, jax.ShapeDtypeStruct(piece.shape, piece.dtype)],
            in_specs=[hbm] * 5 + [anywhere],
            out_specs=[hbm, anywhere],
            input_output_aliases={5: 1},
            scratch_shapes=scalars
            + [
                pltpu.VMEM((fields, rows, width), f32),
                pltpu.VMEM((fields, rows, width), f32),
                pltpu.VMEM((rows, width), f32),
                pltpu.VMEM((2, fields, rows, width), f32),
                pltpu.SemaphoreType.DMA((5,)),
            ],
            compiler_params=limit,
        )(advection, coupling, state_now, time_source, viscosity, piece)
        insides.append(inside)
        return piece

    even, odd = spread(table, blocks, sz.first - 1, interior)
    work = [
        pltpu.VMEM((blocks, fields, SUB, LANES), f32),
        pltpu.VMEM((sz.packs, SUB, fields, SUB, LANES), f32),
        pltpu.VMEM((sz.packs, sz.groups, fields, SUB, LANES), f32),
        pltpu.VMEM((sz.packs, sz.groups, fields, SUB, LANES), f32),
        pltpu.VMEM((sz.packs, fields, SUB, width), f32),
        pltpu.VMEM((fields, blocks, width), f32),
    ]
    carried = [
        pltpu.VMEM((blocks, SUB, LANES), i32),
        pltpu.VMEM((blocks, SUB, LANES), f32),
        pltpu.VMEM((SUB, LANES), i32),
        pltpu.VMEM((SUB, LANES), f32),
        pltpu.VMEM((sz.packs, SUB, width), i32),
        pltpu.VMEM((sz.packs, SUB, width), i32),
        pltpu.VMEM((blocks, blocks), f32),
        pltpu.VMEM((4, sz.packs, SUB, width), f32),
        pltpu.VMEM((2, sz.packs, fields, SUB, width), f32),
        pltpu.VMEM((2, fields, SUB, width), f32),
    ]
    return pl.pallas_call(
        functools.partial(couple_kernel, sz),
        out_shape=block,
        in_specs=[smem] + [hbm] * 3 + [vmem] * 2 + [hbm],
        out_specs=hbm,
        input_output_aliases={6: 0},
        scratch_shapes=scalars + [visc_ends, two_ends, pltpu.SemaphoreType.DMA((6,))] + carried + work,
        compiler_params=limit,
    )(me, advection, coupling, viscosity, even, odd, insides[0])


def solution(mesh):
    return jax.shard_map(
        per_device,
        mesh=mesh,
        in_specs=(
            P(None, None, ("groups", "blk")),
            P(None, None, ("groups", "blk")),
            P(None, ("groups", "blk")),
            P(),
            P(),
            P(("groups", "blk"), None),
            P(("groups", "blk")),
            P(("groups", "blk")),
            P(("groups", "blk")),
        ),
        out_specs=P(None, None, ("groups", "blk")),
        check_vma=False,
    )
```
